512 devices in a mesh: section: 64 (over x, z, y_hi), tp: 8 (over y_lo, core).
Axes of the slice: x: 4, y: 8 (y_hi: 2, y_lo: 4; y = y_hi * 4 + y_lo), z: 8, core: 2. Of those that a mesh axis runs over, the one named last changes fastest.
Arguments:
- hidden_in: bfloat16 [8192, 8192], P('section', 'tp')
- grad_sent: bfloat16 [8192, 8192], P('section', 'tp'), may hold values from -1.25 to 1.25
- value_grad: bfloat16 [8192, 1024], P('section', 'tp'), may hold values from -4 to 4
- value_weight: bfloat16 [524288, 1024], P('section', 'tp'), may hold values from -0.0625 to 0.0625
- rotation: bfloat16 [8192, 1024], P('section', 'tp'), may hold values from -0.5 to 0.5
- act_scale: float32 [64, 8192], P('section', 'tp'), may hold values from 0.1 to 0.6
- outliers: int32 [64, 128], P('section'), may hold values from 0 to 8191, as said below
Outputs:
- emitted: bfloat16 [8192, 8192], P('section', 'tp')
- r1_grad: float32 [4096, 8192], P('tp', 'section')
- r2_grad: float32 [8192, 1024], P('section', 'tp')
The draws below stay inside these ranges and needn't reach their ends.
Inputs may be any that keep to these rules, and one draw needn't show every extreme that they name: `outliers`: each row holds 128 distinct column indices.
All inputs are finite; a program needn't handle non-finite values.
Results may differ from the reference program's by a relative error of at most 0.019.
Values may be sent and summed in bfloat16 or wider, within the bound.
No kernel may reach another device: no remote copies, remote signals or barrier semaphores. Data moves between devices by JAX's collectives and lax.ppermute only.
A program may use at most 64 MiB of HBM per device.

```python
import math
import jax
import jax.numpy as jnp
from jax import lax

D = 8192
KVH = 8
HD = 128
TOK = 128
OUT_K = 128
ROWS_OUT = 4096
SECTIONS = 64
N_TP = 8


def draw_hidden_in(key, part):
    key = jax.random.fold_in(key, 11)
    base_key, row_key = jax.random.split(key, 2)
    row_total = SECTIONS * TOK
    column_pos = jnp.arange(D, dtype=jnp.float32)[None, :] / (D - 1)
    base = jax.random.normal(base_key, (row_total, D), jnp.float32)
    spread = jax.random.uniform(row_key, (row_total, 1), jnp.float32, 0.0, math.log(10.0))
    ramp = jnp.exp(math.log(2.45) * column_pos)
    return (base * ramp * jnp.exp(spread)).astype(jnp.bfloat16)


def draw_outliers(key, part):
    key = jax.random.fold_in(key, 23)
    section_keys = jax.random.split(key, SECTIONS)
    orders = jax.vmap(lambda one_key: jax.random.permutation(one_key, D))(section_keys).astype(jnp.int32)
    section_ids = jnp.arange(SECTIONS, dtype=jnp.int32)
    target = jnp.where(section_ids == 0, D - 1, jnp.where(section_ids == SECTIONS - 1, 0, -1)).astype(jnp.int32)
    position = jnp.argmax(orders == target[:, None], axis=1).astype(jnp.int32)
    first_val = orders[:, 0]
    found_val = jnp.take_along_axis(orders, position[:, None], axis=1)[:, 0]
    column_ids = jnp.arange(D, dtype=jnp.int32)[None, :]
    swapped = jnp.where(column_ids == position[:, None], first_val[:, None], orders)
    swapped = jnp.where(column_ids == 0, found_val[:, None], swapped)
    return swapped[:, :OUT_K].astype(jnp.int32)


def level_of(key, extent, cuts, low, top_value):
    factor_of = 1.0
    for dim, parts in cuts:
        draws = jax.random.uniform(jax.random.fold_in(jax.random.fold_in(key, 6), dim), (parts,), jnp.float32, low / len(cuts), top_value / len(cuts))
        factor_of = factor_of * jnp.repeat(jnp.exp(draws), extent[dim] // parts).reshape((-1,) + (1,) * (len(extent) - 1 - dim))
    return factor_of


def bell_draw(key, dims, width, bound, cuts=(), kind=jnp.bfloat16):
    array = jax.random.normal(key, dims, jnp.float32) * width
    if len(cuts) > 0:
        array = level_of(key, dims, cuts, -0.22, 0.18) * array
    return jnp.clip(array, min=-bound, max=bound).astype(kind)


def setup_inputs(seed: int = 0) -> dict:
    arg_keys = jax.random.split(jax.random.key(seed), 8)
    hidden_in = draw_hidden_in(jax.random.fold_in(arg_keys[7], 71), 0)
    grad_sent = bell_draw(arg_keys[1], (SECTIONS * TOK, D), 0.08, 1.25, ((0, 64), (1, 8)))
    value_grad = bell_draw(arg_keys[2], (SECTIONS * TOK, KVH * HD), 0.25, 4.0, ((0, 64), (1, 8)))
    value_weight = bell_draw(arg_keys[3], (SECTIONS * D, KVH * HD), D ** -0.5, 0.0625, ((0, 64), (1, 8)))
    rotation = bell_draw(arg_keys[4], (SECTIONS * HD, KVH * HD), HD ** -0.5, 0.5, ((0, 64), (1, 8)))
    act_scale = jnp.clip(jnp.exp(math.log(0.6) - 1.7917595 * jax.random.uniform(arg_keys[5], (SECTIONS, D), jnp.float32) ** level_of(arg_keys[5], (SECTIONS, D), ((0, 64), (1, 8)), -0.2, 0.2)), 0.1, 0.6)
    outliers = draw_outliers(jax.random.fold_in(arg_keys[7], 71), 0)
    return {"hidden_in": hidden_in, "grad_sent": grad_sent, "value_grad": value_grad, "value_weight": value_weight, "rotation": rotation, "act_scale": act_scale, "outliers": outliers}


NORM_EPS = 1e-05
SCALE_FLOOR = 1e-06
TWO_PI = 2.0 * math.pi

def soft_quant(values, step_size):
    scaled = values / step_size
    shifted = scaled - jnp.sin(TWO_PI * scaled) / TWO_PI
    return step_size * 7.0 * jnp.tanh(shifted / 7.0)

def clip_slope(values, step_size):
    bounded = jnp.tanh(values / (7.0 * step_size))
    return 1.0 - bounded * bounded

def reference(hidden_in, grad_sent, value_grad, value_weight, rotation, act_scale, outliers):
    heads_group = KVH // N_TP

    def one_section(section_index):
        stream = lax.dynamic_slice_in_dim(hidden_in, section_index * TOK, TOK, 0).astype(jnp.float32)
        following = ((section_index + 1) % SECTIONS).astype(jnp.int32)
        arriving = lax.dynamic_slice_in_dim(grad_sent, following * TOK, TOK, 0).astype(jnp.float32)
        step_row = lax.dynamic_slice_in_dim(act_scale, section_index, 1, 0)
        outlier_cols = lax.dynamic_slice_in_dim(outliers, section_index, 1, 0)[0]
        weights = lax.dynamic_slice_in_dim(value_weight, section_index * D, D, 0)
        rotor_block = lax.dynamic_slice_in_dim(rotation, section_index * HD, HD, 0)
        value_block = lax.dynamic_slice_in_dim(value_grad, section_index * TOK, TOK, 0)
        inverse = lax.rsqrt(lax.optimization_barrier(jnp.mean(stream * stream, axis=1, keepdims=True)) + NORM_EPS)
        normed = stream * inverse
        column_ids = jnp.arange(D, dtype=jnp.int32)
        outlier_mask = jnp.any(column_ids[:, None] == outlier_cols[None, :], axis=1)[None, :]
        quant = jnp.where(outlier_mask, normed, soft_quant(normed, step_row)).astype(jnp.bfloat16)
        weight_heads = weights.reshape(D, KVH, HD).astype(jnp.float32)
        rotor_heads = rotor_block.reshape(HD, KVH, HD).astype(jnp.float32)
        rotated = jnp.einsum('dhk,khj->dhj', weight_heads, rotor_heads).astype(jnp.bfloat16)
        wstep = lax.optimization_barrier(jnp.max(jnp.abs(rotated.astype(jnp.float32)), axis=0)) / 7.0 + SCALE_FLOOR
        wquant = soft_quant(rotated.astype(jnp.float32), wstep).astype(jnp.bfloat16)
        value_heads = value_block.astype(jnp.float32).reshape(TOK, N_TP, heads_group, HD)
        wquant_groups = wquant.astype(jnp.float32).reshape(D, N_TP, heads_group, HD)
        group_parts = jnp.einsum('ngpj,dgpj->gnd', value_heads, wquant_groups).astype(jnp.bfloat16)
        quant_grad = lax.optimization_barrier(jnp.sum(group_parts.astype(jnp.float32), axis=0))
        normed_grad = jnp.where(outlier_mask, quant_grad, quant_grad * clip_slope(normed, step_row))
        emitted_block = (arriving + inverse * normed_grad).astype(jnp.bfloat16)
        slab = rotated[:ROWS_OUT].astype(jnp.float32).reshape(ROWS_OUT, N_TP, heads_group, HD)
        frame_parts = jnp.einsum('ngpj,rgpj->gnr', value_heads, slab).astype(jnp.bfloat16)
        frame = lax.optimization_barrier(jnp.sum(frame_parts.astype(jnp.float32), axis=0)).astype(jnp.bfloat16)
        projected = jnp.dot(quant, weights, preferred_element_type=jnp.float32).reshape(TOK, KVH, HD)
        rotation_grad = jnp.einsum('nhk,nhj->khj', projected, value_block.astype(jnp.float32).reshape(TOK, KVH, HD), precision=lax.Precision.HIGHEST)
        return (emitted_block, rotation_grad.reshape(HD, KVH * HD), frame, quant)
    emitted_all, rotation_all, frame_all, quant_all = lax.map(one_section, jnp.arange(SECTIONS, dtype=jnp.int32))
    emitted = emitted_all.reshape(SECTIONS * TOK, D)
    r2_grad = rotation_all.reshape(SECTIONS * HD, KVH * HD)
    frame_rows = frame_all.reshape(SECTIONS * TOK, ROWS_OUT)
    quant_rows = quant_all.reshape(SECTIONS * TOK, D)
    r1_grad = jnp.dot(frame_rows.T, quant_rows, preferred_element_type=jnp.float32)
    return (emitted, r1_grad, r2_grad)
```

```python
import math

import jax
import jax.numpy as jnp
from jax import lax
from jax.experimental import pallas as pl
from jax.experimental.pallas import tpu as pltpu
from jax.sharding import Mesh
from jax.sharding import PartitionSpec as P

ROWS_OUT = 4096
NORM_EPS = 1e-05
SCALE_FLOOR = 1e-06
TP = 8
BIG = 32 << 20
CHEAP = pl.CostEstimate(flops=1, bytes_accessed=1, transcendentals=0)
LONG = pl.CostEstimate(flops=9_000_000_000, bytes_accessed=1, transcendentals=0)
SEC = ("x", "zh", "zl", "yh")
TPA = ("yl", "c")
NEAR = ("x", "zl")
FAR = ("zh", "yh")
SIN_POLY = (
    0.9999995827674866,
    -6.579691410064697,
    12.986435890197754,
    -12.188101768493652,
    6.558041572570801,
    -1.9530311822891235,
)


def soft_quant(values, inv_step, step7):
    scaled = values * inv_step
    turn = scaled - jnp.round(scaled)
    square = turn * turn
    poly = SIN_POLY[-1]
    for coef in SIN_POLY[-2::-1]:
        poly = poly * square + coef
    shifted = scaled - turn * poly
    return step7 * jnp.tanh(shifted * (1.0 / 7.0))


def dot_nt(left, right):
    return lax.dot_general(
        left, right, (((1,), (1,)), ((), ())), preferred_element_type=jnp.float32
    )


def three_terms(value):
    top = value.astype(jnp.bfloat16).astype(jnp.float32)
    rest = value - top
    mid = rest.astype(jnp.bfloat16).astype(jnp.float32)
    return top, mid, rest - mid


def prepare_kernel(x_ref, scale_ref, out_ref):
    squares = jnp.zeros((128, 128), jnp.float32)
    for lane in range(8):
        x = x_ref[:, lane * 128 : (lane + 1) * 128].astype(jnp.float32)
        squares += x * x
    squares = jnp.sum(jnp.transpose(squares), axis=0, keepdims=True)
    squares = jnp.concatenate([squares] + [jnp.zeros((1, 896), jnp.float32)], axis=1)
    row = lax.broadcasted_iota(jnp.int32, (16, 1024), 0)
    extra = jnp.zeros((16, 1024), jnp.float32)
    for index, term in enumerate(three_terms(scale_ref[...]) + three_terms(squares)):
        extra = jnp.where(row == index, term, extra)
    extra = extra.astype(jnp.bfloat16)
    for copy in range(4):
        out_ref[copy, 0:128, :] = x_ref[...]
        out_ref[copy, 128:144, :] = extra


def prepare(hidden, scale):
    return pl.pallas_call(
        prepare_kernel,
        out_shape=jax.ShapeDtypeStruct((4, 144, 1024), jnp.bfloat16),
        compiler_params=pltpu.CompilerParams(vmem_limit_bytes=BIG),
        cost_estimate=CHEAP,
        name="prepare",
    )(hidden, scale)


def rotate_kernel(core_ref, w_ref, r2_ref, dv_ref, rot_ref, top_ref, keep_ref, send_ref):
    step = pl.program_id(0)
    core = core_ref[0]
    rot = jnp.dot(w_ref[...], r2_ref[...], preferred_element_type=jnp.float32).astype(jnp.bfloat16)
    rot_ref[...] = rot
    top = jnp.max(jnp.abs(rot.astype(jnp.float32)), axis=0, keepdims=True)

    @pl.when(step == 0)
    def _():
        top_ref[...] = top

    @pl.when(step > 0)
    def _():
        top_ref[...] = jnp.maximum(top_ref[...], top)

    @pl.when(step < 2)
    def _():
        for part in range(4):
            prod = dot_nt(dv_ref[...], rot[part * 512 : (part + 1) * 512]).astype(jnp.bfloat16)
            chip = (step * 2 + part // 2 + 4 - core_ref[1]) % 4

            @pl.when(core == part % 2)
            def _():
                keep_ref[chip] = prod

            @pl.when(core != part % 2)
            def _():
                send_ref[chip] = prod


def rotate(core, weight, rotor, value_grad):
    whole = lambda i, core: (0, 0)
    block = lambda i, core: (i, 0)
    half = jax.ShapeDtypeStruct((4, 128, 512), jnp.bfloat16)
    return pl.pallas_call(
        rotate_kernel,
        grid_spec=pltpu.PrefetchScalarGridSpec(
            num_scalar_prefetch=1,
            grid=(4,),
            in_specs=[
                pl.BlockSpec((2048, 128), block),
                pl.BlockSpec((128, 128), whole),
                pl.BlockSpec((128, 128), whole),
            ],
            out_specs=[
                pl.BlockSpec((2048, 128), block),
                pl.BlockSpec((1, 128), whole),
                pl.BlockSpec((4, 128, 512), lambda i, core: (0, 0, 0)),
                pl.BlockSpec((4, 128, 512), lambda i, core: (0, 0, 0)),
            ],
        ),
        out_shape=[
            jax.ShapeDtypeStruct((8192, 128), jnp.bfloat16),
            jax.ShapeDtypeStruct((1, 128), jnp.float32),
            half,
            half,
        ],
        compiler_params=pltpu.CompilerParams(vmem_limit_bytes=BIG),
        cost_estimate=pl.CostEstimate(flops=23000000000, bytes_accessed=1, transcendentals=0),
        name="rotate",
    )(core, weight, rotor, value_grad)


def weight_grad_kernel(core_ref, rot_ref, top_ref, dv_ref, send_ref, keep_ref):
    index = pl.program_id(0)
    step = top_ref[...] / 7.0 + SCALE_FLOOR
    quant = soft_quant(rot_ref[...].astype(jnp.float32), 1.0 / step, step * 7.0)
    prod = dot_nt(dv_ref[...], quant.astype(jnp.bfloat16)).astype(jnp.bfloat16)

    @pl.when(index < 4)
    def _():
        send_ref[0] = prod

    @pl.when(index >= 4)
    def _():
        keep_ref[0] = prod


def weight_grad(core, rot, top, value_grad):
    half = jax.ShapeDtypeStruct((4, 128, 1024), jnp.bfloat16)
    return pl.pallas_call(
        weight_grad_kernel,
        grid_spec=pltpu.PrefetchScalarGridSpec(
            num_scalar_prefetch=1,
            grid=(8,),
            in_specs=[
                pl.BlockSpec(
                    (1024, 128),
                    lambda i, core: (
                        ((i + core[1]) % 4) * 2 + jnp.where(i < 4, 1 - core[0], core[0]),
                        0,
                    ),
                ),
                pl.BlockSpec((1, 128), lambda i, core: (0, 0)),
                pl.BlockSpec((128, 128), lambda i, core: (0, 0)),
            ],
            out_specs=[
                pl.BlockSpec((1, 128, 1024), lambda i, core: (jnp.minimum(i, 3), 0, 0)),
                pl.BlockSpec((1, 128, 1024), lambda i, core: (jnp.maximum(i - 4, 0), 0, 0)),
            ],
        ),
        out_shape=[half, half],
        compiler_params=pltpu.CompilerParams(vmem_limit_bytes=BIG),
        cost_estimate=pl.CostEstimate(flops=10350000000, bytes_accessed=1, transcendentals=0),
        name="weight_grad",
    )(core, rot, top, value_grad)


def quant_kernel(core_ref, all_ref, mask_ref, inv_ref, quant_ref):
    inverse = jnp.transpose(jnp.broadcast_to(inv_ref[...], (128, 128)))
    mask = mask_ref[0]
    scale = all_ref[0, 128:144, :].astype(jnp.float32)
    scale = scale[0:1] + scale[1:2] + scale[2:3]
    recip = 1.0 / scale
    scale7 = scale * 7.0
    for lane in range(8):
        cols = slice(lane * 128, (lane + 1) * 128)
        normed = all_ref[0, 0:128, cols].astype(jnp.float32) * inverse
        soft = soft_quant(normed, recip[:, cols], scale7[:, cols])
        quant = jnp.where(mask[:, cols] > 0.0, normed, soft).astype(jnp.bfloat16)
        zh, zl, yh = lane // 4, (lane // 2) % 2, lane % 2
        place = zh * 2 + yh
        quant_ref[zl, :, place * 128 : (place + 1) * 128] = quant


def quantize(core, hidden_all, mask, inverse):
    return pl.pallas_call(
        quant_kernel,
        grid_spec=pltpu.PrefetchScalarGridSpec(
            num_scalar_prefetch=1,
            grid=(4,),
            in_specs=[
                pl.BlockSpec((1, 144, 1024), lambda i, core: (i, 0, 0)),
                pl.BlockSpec((1, 1, 1024), lambda i, core: (i * 2 + core[0], 0, 0)),
                pl.BlockSpec((1, 128), lambda i, core: (0, 0)),
            ],
            out_specs=pl.BlockSpec((2, 128, 512), lambda i, core: (i, 0, 0)),
        ),
        out_shape=jax.ShapeDtypeStruct((8, 128, 512), jnp.bfloat16),
        compiler_params=pltpu.CompilerParams(vmem_limit_bytes=BIG),
        cost_estimate=CHEAP,
        name="quantize",
    )(core, hidden_all, mask, inverse)


def rotor_grad_kernel(core_ref, mine_ref, other_ref, wm_ref, wo_ref, dv_ref, r2_ref, total_ref):
    step = pl.program_id(0)
    total = jnp.zeros((128, 128), jnp.float32)
    for quant_ref, weight_ref in ((mine_ref, wm_ref), (other_ref, wo_ref)):
        for lane in range(8):
            zh, zl, yh = lane // 4, (lane // 2) % 2, lane % 2
            place = zh * 2 + yh
            total += jnp.dot(
                quant_ref[zl, :, place * 128 : (place + 1) * 128],
                weight_ref[0, lane * 128 : (lane + 1) * 128, :],
                preferred_element_type=jnp.float32,
            )

    @pl.when(step == 0)
    def _():
        total_ref[...] = total

    @pl.when(step > 0)
    def _():
        total_ref[...] += total

    @pl.when(step == 3)
    def _():
        r2_ref[...] = lax.dot_general(
            total_ref[...],
            dv_ref[...].astype(jnp.float32),
            (((0,), (0,)), ((), ())),
            precision=lax.Precision.HIGHEST,
            preferred_element_type=jnp.float32,
        )


def rotor_grad(core, mine, other, weight, value_grad):
    weight = weight.reshape(8, 1024, 128)
    quant_spec = pl.BlockSpec((2, 128, 512), lambda i, core: (i, 0, 0))
    return pl.pallas_call(
        rotor_grad_kernel,
        grid_spec=pltpu.PrefetchScalarGridSpec(
            num_scalar_prefetch=1,
            grid=(4,),
            in_specs=[
                quant_spec,
                quant_spec,
                pl.BlockSpec((1, 1024, 128), lambda i, core: (i * 2 + core[0], 0, 0)),
                pl.BlockSpec((1, 1024, 128), lambda i, core: (i * 2 + 1 - core[0], 0, 0)),
                pl.BlockSpec((128, 128), lambda i, core: (0, 0)),
            ],
            out_specs=pl.BlockSpec((128, 128), lambda i, core: (0, 0)),
            scratch_shapes=[pltpu.VMEM((128, 128), jnp.float32)],
        ),
        out_shape=jax.ShapeDtypeStruct((128, 128), jnp.float32),
        compiler_params=pltpu.CompilerParams(vmem_limit_bytes=BIG),
        cost_estimate=CHEAP,
        name="rotor_grad",
    )(core, mine, other, weight, weight, value_grad)


def outer_kernel(place_ref, frame_ref, mine_ref, other_ref, out_ref, left_ref):
    x, zl, yh = place_ref[2], place_ref[3], place_ref[4]

    @pl.when(pl.program_id(0) == 0)
    def _():
        for near in range(8):
            turn = (near // 2 + 4 - x) % 4
            flip = (near % 2 + zl) % 2
            left_ref[near * 128 : (near + 1) * 128, :] = frame_ref[turn * 2 + flip]

    def product(quant_ref):
        prod = lax.dot_general(
            left_ref[...],
            quant_ref[...],
            (((0,), (0,)), ((), ())),
            preferred_element_type=jnp.float32,
        ).astype(jnp.bfloat16)
        for part in range(2):
            out_ref[(part + yh) % 2] = prod[:, part * 128 : (part + 1) * 128]

    @pl.when(pl.program_id(0) < 2)
    def _():
        product(mine_ref)

    @pl.when(pl.program_id(0) >= 2)
    def _():
        product(other_ref)


def outer(place, frames, mine, other):
    return pl.pallas_call(
        outer_kernel,
        grid_spec=pltpu.PrefetchScalarGridSpec(
            num_scalar_prefetch=1,
            grid=(4,),
            in_specs=[
                pl.BlockSpec((8, 128, 512), lambda i, place: (0, 0, 0)),
                pl.BlockSpec((1024, 256), lambda i, place: (0, jnp.minimum(i, 1))),
                pl.BlockSpec((1024, 256), lambda i, place: (0, jnp.maximum(i - 2, 0))),
            ],
            out_specs=pl.BlockSpec(
                (2, 512, 128),
                lambda i, place: (jnp.where(i < 2, place[0], 1 - place[0]) * 2 + i % 2, 0, 0),
            ),
            scratch_shapes=[pltpu.VMEM((1024, 512), jnp.bfloat16)],
        ),
        out_shape=jax.ShapeDtypeStruct((8, 512, 128), jnp.bfloat16),
        compiler_params=pltpu.CompilerParams(vmem_limit_bytes=BIG),
        cost_estimate=CHEAP,
        name="outer",
    )(place, frames, mine, other)


def exchange(value, axes):
    return lax.all_to_all(value, axes, split_axis=0, concat_axis=0, tiled=True)


def shifted(value, axis, turn):
    count = lax.axis_size(axis)
    return lax.ppermute(value, axis, [(chip, (chip + turn) % count) for chip in range(count)])


def swap_core(value):
    return shifted(value, "c", 1)


def local(hidden_in, grad_sent, value_grad, value_weight, rotation, act_scale, outliers):
    sections = 64
    pairs = [(source, (source - 1) % sections) for source in range(sections)]
    place = jnp.stack([lax.axis_index(axis) for axis in ("c", "yl", "x", "zl", "yh")])
    place = place.astype(jnp.int32)
    wide = lambda value: value.astype(jnp.float32)
    tie = lax.optimization_barrier

    def chip_sum(pair):
        total = pair[0]
        for turn in (1, 2, 3):
            total = total + wide(shifted(pair[turn].astype(jnp.bfloat16), "yl", turn))
        return total

    hidden_all = exchange(prepare(hidden_in, act_scale), "yl")

    rot, peak, frame_keep, frame_send = rotate(place, value_weight, rotation, value_grad)
    frame_recv = swap_core(frame_send)
    frame = chip_sum([wide(frame_keep[turn]) + wide(frame_recv[turn]) for turn in range(4)])
    frame = frame.astype(jnp.bfloat16)
    grad_send, grad_keep = weight_grad(place, rot, peak, value_grad)
    hidden_all, frame, grad_send, grad_keep, grad_sent = tie(
        (hidden_all, frame, grad_send, grad_keep, grad_sent)
    )
    pair = jnp.stack([frame, shifted(frame, "zl", 1)])
    ids = outliers[0]
    blocks = (ids[None, :] // 128 == jnp.arange(64)[:, None]).astype(jnp.bfloat16)
    lanes = (ids[:, None] % 128 == jnp.arange(128)[None, :]).astype(jnp.bfloat16)
    mask = jnp.dot(blocks, lanes, preferred_element_type=jnp.float32).reshape(TP, 1, 1024)

    squares = jnp.sum(wide(hidden_all[:, 131:134, :128]), axis=(0, 1)).reshape(1, 128)
    inverse = lax.rsqrt((squares + swap_core(squares)) / 8192.0 + NORM_EPS)
    quant = quantize(place, hidden_all, mask, inverse)
    quant, pair = tie((quant, pair))
    quants = exchange(quant, NEAR)
    before, after = shifted(pair, "x", 1), shifted(pair, "x", -1)
    across = jnp.concatenate([shifted(before[:, :64], "x", 1), shifted(after[:, 64:], "x", -1)], 1)
    frames = jnp.concatenate([pair, after, across, before])
    incoming = lax.ppermute(grad_sent, SEC, pairs)
    quants, frames, incoming, quant, grad_send, grad_keep = tie(
        (quants, frames, incoming, quant, grad_send, grad_keep)
    )
    quants_other = swap_core(quants)
    parts = outer(place, frames, quants.reshape(1024, 512), quants_other.reshape(1024, 512))
    r2_grad = rotor_grad(place, quant, swap_core(quant), value_weight, value_grad)
    grad_recv = swap_core(grad_send)
    grad_sum = chip_sum([wide(grad_keep[turn]) + wide(grad_recv[turn]) for turn in range(4)])
    parts = exchange(parts, "zh").reshape(4, 2, 512, 128)
    sums = jnp.sum(wide(parts), axis=0)
    r1_grad = sums[0] + wide(shifted(sums[1].astype(jnp.bfloat16), "yh", 1))

    mask_mine = lax.dynamic_index_in_dim(mask, lax.axis_index(TPA), 0, keepdims=False)
    inverse = inverse.reshape(128, 1)
    normed = wide(hidden_in) * inverse
    bounded = jnp.tanh(normed / (7.0 * act_scale))
    slope = jnp.where(mask_mine > 0.0, 1.0, 1.0 - bounded * bounded)
    emitted = (wide(incoming) + inverse * (grad_sum * slope)).astype(jnp.bfloat16)
    return (emitted, r1_grad, r2_grad)


def solution(mesh):
    fine = Mesh(mesh.devices.reshape(4, 4, 2, 2, 4, 2), SEC + TPA)
    both = P(SEC, TPA)
    in_specs = (both, both, both, both, both, both, P(SEC, None))
    out_specs = (both, P(TPA, SEC), both)
    return jax.shard_map(local, mesh=fine, in_specs=in_specs, out_specs=out_specs, check_vma=False)
```

```python
import math

import jax
import jax.numpy as jnp
from jax import lax
from jax.experimental import pallas as pl
from jax.experimental.pallas import tpu as pltpu
from jax.sharding import Mesh
from jax.sharding import PartitionSpec as P

ROWS_OUT = 4096
NORM_EPS = 1e-05
SCALE_FLOOR = 1e-06
TP = 8
BIG = 32 << 20
CHEAP = pl.CostEstimate(flops=1, bytes_accessed=1, transcendentals=0)
LONG = pl.CostEstimate(flops=23_000_000_000, bytes_accessed=1, transcendentals=0)
SEC = ("x", "zh", "zl", "yh")
TPA = ("yl", "c")
NEAR = ("x", "zl")
FAR = ("zh", "yh")
SIN_POLY = (
    0.9999995827674866,
    -6.579691410064697,
    12.986435890197754,
    -12.188101768493652,
    6.558041572570801,
    -1.9530311822891235,
)


def soft_quant(values, inv_step, step7):
    scaled = values * inv_step
    turn = scaled - jnp.round(scaled)
    square = turn * turn
    poly = SIN_POLY[-1]
    for coef in SIN_POLY[-2::-1]:
        poly = poly * square + coef
    shifted = scaled - turn * poly
    return step7 * jnp.tanh(shifted * (1.0 / 7.0))


def dot_nt(left, right):
    return lax.dot_general(
        left, right, (((1,), (1,)), ((), ())), preferred_element_type=jnp.float32
    )


def prepare_kernel(x_ref, scale_ref, out_ref):
    scale = scale_ref[...]
    top = scale.astype(jnp.bfloat16).astype(jnp.float32)
    rest = scale - top
    mid = rest.astype(jnp.bfloat16).astype(jnp.float32)
    low = rest - mid
    row = lax.broadcasted_iota(jnp.int32, (16, scale.shape[1]), 0)
    extra = jnp.where(row == 0, top, jnp.where(row == 1, mid, jnp.where(row == 2, low, 0.0)))
    out_ref[0:128, :] = x_ref[...]
    out_ref[128:144, :] = extra.astype(jnp.bfloat16)


def prepare(hidden, scale):
    return pl.pallas_call(
        prepare_kernel,
        out_shape=jax.ShapeDtypeStruct((144, 1024), jnp.bfloat16),
        compiler_params=pltpu.CompilerParams(vmem_limit_bytes=BIG),
        cost_estimate=CHEAP,
        name="prepare",
    )(hidden, scale)


def rotate_kernel(core_ref, w_ref, r2_ref, dv_ref, rot_ref, top_ref, keep_ref, send_ref):
    step = pl.program_id(0)
    core = core_ref[0]
    rot = jnp.dot(w_ref[...], r2_ref[...], preferred_element_type=jnp.float32).astype(jnp.bfloat16)
    rot_ref[...] = rot
    top = jnp.max(jnp.abs(rot.astype(jnp.float32)), axis=0, keepdims=True)

    @pl.when(step == 0)
    def _():
        top_ref[...] = top

    @pl.when(step > 0)
    def _():
        top_ref[...] = jnp.maximum(top_ref[...], top)

    @pl.when(step < 2)
    def _():
        for part in range(4):
            prod = dot_nt(dv_ref[...], rot[part * 512 : (part + 1) * 512]).astype(jnp.bfloat16)
            chip = step * 2 + part // 2

            @pl.when(core == part % 2)
            def _():
                keep_ref[chip] = prod

            @pl.when(core != part % 2)
            def _():
                send_ref[chip] = prod


def rotate(core, weight, rotor, value_grad):
    whole = lambda i, core: (0, 0)
    block = lambda i, core: (i, 0)
    half = jax.ShapeDtypeStruct((4, 128, 512), jnp.bfloat16)
    return pl.pallas_call(
        rotate_kernel,
        grid_spec=pltpu.PrefetchScalarGridSpec(
            num_scalar_prefetch=1,
            grid=(4,),
            in_specs=[
                pl.BlockSpec((2048, 128), block),
                pl.BlockSpec((128, 128), whole),
                pl.BlockSpec((128, 128), whole),
            ],
            out_specs=[
                pl.BlockSpec((2048, 128), block),
                pl.BlockSpec((1, 128), whole),
                pl.BlockSpec((4, 128, 512), lambda i, core: (0, 0, 0)),
                pl.BlockSpec((4, 128, 512), lambda i, core: (0, 0, 0)),
            ],
        ),
        out_shape=[
            jax.ShapeDtypeStruct((8192, 128), jnp.bfloat16),
            jax.ShapeDtypeStruct((1, 128), jnp.float32),
            half,
            half,
        ],
        compiler_params=pltpu.CompilerParams(vmem_limit_bytes=BIG),
        cost_estimate=LONG,
        name="rotate",
    )(core, weight, rotor, value_grad)


def weight_grad_kernel(rot_ref, top_ref, dv_ref, out_ref):
    step = top_ref[...] / 7.0 + SCALE_FLOOR
    quant = soft_quant(rot_ref[...].astype(jnp.float32), 1.0 / step, step * 7.0)
    out_ref[0] = dot_nt(dv_ref[...], quant.astype(jnp.bfloat16)).astype(jnp.bfloat16)


def weight_grad(rot, top, value_grad):
    return pl.pallas_call(
        weight_grad_kernel,
        grid=(8,),
        in_specs=[
            pl.BlockSpec((1024, 128), lambda i: (i, 0)),
            pl.BlockSpec((1, 128), lambda i: (0, 0)),
            pl.BlockSpec((128, 128), lambda i: (0, 0)),
        ],
        out_specs=pl.BlockSpec((1, 128, 1024), lambda i: (i, 0, 0)),
        out_shape=jax.ShapeDtypeStruct((8, 128, 1024), jnp.bfloat16),
        compiler_params=pltpu.CompilerParams(vmem_limit_bytes=BIG),
        cost_estimate=CHEAP,
        name="weight_grad",
    )(rot, top, value_grad)


def quant_kernel(core_ref, all_ref, mask_ref, inv_ref, quant_ref):
    inverse = jnp.transpose(jnp.broadcast_to(inv_ref[...], (128, 128)))
    mask = mask_ref[0]
    scale = all_ref[0, 128:144, :].astype(jnp.float32)
    scale = scale[0:1] + scale[1:2] + scale[2:3]
    recip = 1.0 / scale
    scale7 = scale * 7.0
    for lane in range(8):
        cols = slice(lane * 128, (lane + 1) * 128)
        normed = all_ref[0, 0:128, cols].astype(jnp.float32) * inverse
        soft = soft_quant(normed, recip[:, cols], scale7[:, cols])
        quant = jnp.where(mask[:, cols] > 0.0, normed, soft).astype(jnp.bfloat16)
        zh, zl, yh = lane // 4, (lane // 2) % 2, lane % 2
        place = zh * 2 + yh
        quant_ref[zl, :, place * 128 : (place + 1) * 128] = quant


def quantize(core, hidden_all, mask, inverse):
    return pl.pallas_call(
        quant_kernel,
        grid_spec=pltpu.PrefetchScalarGridSpec(
            num_scalar_prefetch=1,
            grid=(4,),
            in_specs=[
                pl.BlockSpec((1, 144, 1024), lambda i, core: (i, 0, 0)),
                pl.BlockSpec((1, 1, 1024), lambda i, core: (i * 2 + core[0], 0, 0)),
                pl.BlockSpec((1, 128), lambda i, core: (0, 0)),
            ],
            out_specs=pl.BlockSpec((2, 128, 512), lambda i, core: (i, 0, 0)),
        ),
        out_shape=jax.ShapeDtypeStruct((8, 128, 512), jnp.bfloat16),
        compiler_params=pltpu.CompilerParams(vmem_limit_bytes=BIG),
        cost_estimate=pl.CostEstimate(flops=10_350_000_000, bytes_accessed=1, transcendentals=0),
        name="quantize",
    )(core, hidden_all, mask, inverse)


def rotor_grad_kernel(core_ref, mine_ref, other_ref, wm_ref, wo_ref, dv_ref, r2_ref, total_ref):
    step = pl.program_id(0)
    total = jnp.zeros((128, 128), jnp.float32)
    for quant_ref, weight_ref in ((mine_ref, wm_ref), (other_ref, wo_ref)):
        for lane in range(8):
            zh, zl, yh = lane // 4, (lane // 2) % 2, lane % 2
            place = zh * 2 + yh
            total += jnp.dot(
                quant_ref[zl, :, place * 128 : (place + 1) * 128],
                weight_ref[0, lane * 128 : (lane + 1) * 128, :],
                preferred_element_type=jnp.float32,
            )

    @pl.when(step == 0)
    def _():
        total_ref[...] = total

    @pl.when(step > 0)
    def _():
        total_ref[...] += total

    @pl.when(step == 3)
    def _():
        r2_ref[...] = lax.dot_general(
            total_ref[...],
            dv_ref[...].astype(jnp.float32),
            (((0,), (0,)), ((), ())),
            precision=lax.Precision.HIGHEST,
            preferred_element_type=jnp.float32,
        )


def rotor_grad(core, mine, other, weight, value_grad):
    weight = weight.reshape(8, 1024, 128)
    quant_spec = pl.BlockSpec((2, 128, 512), lambda i, core: (i, 0, 0))
    return pl.pallas_call(
        rotor_grad_kernel,
        grid_spec=pltpu.PrefetchScalarGridSpec(
            num_scalar_prefetch=1,
            grid=(4,),
            in_specs=[
                quant_spec,
                quant_spec,
                pl.BlockSpec((1, 1024, 128), lambda i, core: (i * 2 + core[0], 0, 0)),
                pl.BlockSpec((1, 1024, 128), lambda i, core: (i * 2 + 1 - core[0], 0, 0)),
                pl.BlockSpec((128, 128), lambda i, core: (0, 0)),
            ],
            out_specs=pl.BlockSpec((128, 128), lambda i, core: (0, 0)),
            scratch_shapes=[pltpu.VMEM((128, 128), jnp.float32)],
        ),
        out_shape=jax.ShapeDtypeStruct((128, 128), jnp.float32),
        compiler_params=pltpu.CompilerParams(vmem_limit_bytes=BIG),
        cost_estimate=CHEAP,
        name="rotor_grad",
    )(core, mine, other, weight, weight, value_grad)


def outer_kernel(place_ref, frame_ref, mine_ref, other_ref, out_ref):
    yh = place_ref[1]

    def product(quant_ref):
        prod = lax.dot_general(
            frame_ref[...],
            quant_ref[...],
            (((0,), (0,)), ((), ())),
            preferred_element_type=jnp.float32,
        ).astype(jnp.bfloat16)
        for part in range(2):
            out_ref[(part + yh) % 2] = prod[:, part * 128 : (part + 1) * 128]

    @pl.when(pl.program_id(0) < 2)
    def _():
        product(mine_ref)

    @pl.when(pl.program_id(0) >= 2)
    def _():
        product(other_ref)


def outer(place, frames, mine, other):
    return pl.pallas_call(
        outer_kernel,
        grid_spec=pltpu.PrefetchScalarGridSpec(
            num_scalar_prefetch=1,
            grid=(4,),
            in_specs=[
                pl.BlockSpec((1024, 512), lambda i, place: (0, 0)),
                pl.BlockSpec((1024, 256), lambda i, place: (0, jnp.minimum(i, 1))),
                pl.BlockSpec((1024, 256), lambda i, place: (0, jnp.maximum(i - 2, 0))),
            ],
            out_specs=pl.BlockSpec(
                (2, 512, 128),
                lambda i, place: (jnp.where(i < 2, place[0], 1 - place[0]) * 2 + i % 2, 0, 0),
            ),
        ),
        out_shape=jax.ShapeDtypeStruct((8, 512, 128), jnp.bfloat16),
        compiler_params=pltpu.CompilerParams(vmem_limit_bytes=BIG),
        cost_estimate=CHEAP,
        name="outer",
    )(place, frames, mine, other)


def exchange(value, axes):
    return lax.all_to_all(value, axes, split_axis=0, concat_axis=0, tiled=True)


def shifted(value, axis, turn):
    count = lax.axis_size(axis)
    return lax.ppermute(value, axis, [(chip, (chip + turn) % count) for chip in range(count)])


def swap_core(value):
    return shifted(value, "c", 1)


def local(hidden_in, grad_sent, value_grad, value_weight, rotation, act_scale, outliers):
    sections = 64
    pairs = [(source, (source - 1) % sections) for source in range(sections)]
    place = jnp.stack([lax.axis_index("c"), lax.axis_index("yh")]).astype(jnp.int32)
    wide = lambda value: value.astype(jnp.float32)
    tie = lax.optimization_barrier

    hidden_all = lax.all_gather(prepare(hidden_in, act_scale), "yl", axis=0)

    rot, peak, frame_keep, frame_send = rotate(place, value_weight, rotation, value_grad)
    frame_pair = (wide(frame_keep) + wide(swap_core(frame_send))).astype(jnp.bfloat16)
    rot, frame_pair, hidden_two = tie((rot, frame_pair, hidden_in))
    frame_terms = exchange(frame_pair, "yl")
    squares = jnp.sum(wide(hidden_two) * wide(hidden_two), axis=1).reshape(1, 128)
    squares = squares + swap_core(squares)
    moved = [shifted(squares, "yl", turn) for turn in (1, 2, 3)]
    inverse = lax.rsqrt((squares + moved[0] + moved[1] + moved[2]) / 8192.0 + NORM_EPS)
    frame_terms, inverse, rot = tie((frame_terms, inverse, rot))
    frame = jnp.sum(wide(frame_terms), axis=0).astype(jnp.bfloat16)
    frames = exchange(jnp.broadcast_to(frame[None], (8, 128, 512)), NEAR).reshape(1024, 512)
    grad_parts = weight_grad(rot, peak, value_grad)

    ids = outliers[0]
    blocks = (ids[None, :] // 128 == jnp.arange(64)[:, None]).astype(jnp.bfloat16)
    lanes = (ids[:, None] % 128 == jnp.arange(128)[None, :]).astype(jnp.bfloat16)
    mask = jnp.dot(blocks, lanes, preferred_element_type=jnp.float32).reshape(TP, 1, 1024)

    hidden_all, mask, grad_parts = tie((hidden_all, mask, grad_parts))
    grad_sum = lax.psum_scatter(grad_parts, TPA, scatter_dimension=0, tiled=False)
    quant = quantize(place, hidden_all, mask, inverse)
    frames, quant = tie((frames, quant))
    quants = exchange(quant, NEAR)
    r2_grad = rotor_grad(place, quant, swap_core(quant), value_weight, value_grad)
    quants, r2_grad, grad_sent = tie((quants, r2_grad, grad_sent))
    quants_other = swap_core(quants)
    incoming = lax.ppermute(grad_sent, SEC, pairs)
    parts = outer(place, frames, quants.reshape(1024, 512), quants_other.reshape(1024, 512))
    parts = exchange(parts, "zh").reshape(4, 2, 512, 128)
    sums = jnp.sum(wide(parts), axis=0)
    r1_grad = sums[0] + wide(shifted(sums[1].astype(jnp.bfloat16), "yh", 1))

    mask_mine = lax.dynamic_index_in_dim(mask, lax.axis_index(TPA), 0, keepdims=False)
    inverse = inverse.reshape(128, 1)
    normed = wide(hidden_in) * inverse
    bounded = jnp.tanh(normed / (7.0 * act_scale))
    slope = jnp.where(mask_mine > 0.0, 1.0, 1.0 - bounded * bounded)
    emitted = (wide(incoming) + inverse * (wide(grad_sum) * slope)).astype(jnp.bfloat16)
    return (emitted, r1_grad, r2_grad)


def solution(mesh):
    fine = Mesh(mesh.devices.reshape(4, 4, 2, 2, 4, 2), SEC + TPA)
    both = P(SEC, TPA)
    in_specs = (both, both, both, both, both, both, P(SEC, None))
    out_specs = (both, P(TPA, SEC), both)
    return jax.shard_map(local, mesh=fine, in_specs=in_specs, out_specs=out_specs, check_vma=False)
```

```python
import math

import jax
import jax.numpy as jnp
from jax import lax
from jax.experimental import pallas as pl
from jax.experimental.pallas import tpu as pltpu
from jax.sharding import Mesh
from jax.sharding import PartitionSpec as P

ROWS_OUT = 4096
NORM_EPS = 1e-05
SCALE_FLOOR = 1e-06
TP = 8
BIG = 32 << 20
CHEAP = pl.CostEstimate(flops=1, bytes_accessed=1, transcendentals=0)
LONG = pl.CostEstimate(flops=23_000_000_000, bytes_accessed=1, transcendentals=0)
SEC = ("x", "zh", "zl", "yh")
TPA = ("yl", "c")
NEAR = ("x", "zl")
FAR = ("zh", "yh")
SIN_POLY = (
    0.9999995827674866,
    -6.579691410064697,
    12.986435890197754,
    -12.188101768493652,
    6.558041572570801,
    -1.9530311822891235,
)


def soft_quant(values, inv_step, step7):
    scaled = values * inv_step
    turn = scaled - jnp.round(scaled)
    square = turn * turn
    poly = SIN_POLY[-1]
    for coef in SIN_POLY[-2::-1]:
        poly = poly * square + coef
    shifted = scaled - turn * poly
    return step7 * jnp.tanh(shifted * (1.0 / 7.0))


def dot_nt(left, right):
    return lax.dot_general(
        left, right, (((1,), (1,)), ((), ())), preferred_element_type=jnp.float32
    )


def three_terms(value):
    top = value.astype(jnp.bfloat16).astype(jnp.float32)
    rest = value - top
    mid = rest.astype(jnp.bfloat16).astype(jnp.float32)
    return top, mid, rest - mid


def prepare_kernel(x_ref, scale_ref, out_ref):
    squares = jnp.zeros((128, 128), jnp.float32)
    for lane in range(8):
        x = x_ref[:, lane * 128 : (lane + 1) * 128].astype(jnp.float32)
        squares += x * x
    squares = jnp.sum(jnp.transpose(squares), axis=0, keepdims=True)
    squares = jnp.concatenate([squares] + [jnp.zeros((1, 896), jnp.float32)], axis=1)
    row = lax.broadcasted_iota(jnp.int32, (16, 1024), 0)
    extra = jnp.zeros((16, 1024), jnp.float32)
    for index, term in enumerate(three_terms(scale_ref[...]) + three_terms(squares)):
        extra = jnp.where(row == index, term, extra)
    out_ref[0:128, :] = x_ref[...]
    out_ref[128:144, :] = extra.astype(jnp.bfloat16)


def prepare(hidden, scale):
    return pl.pallas_call(
        prepare_kernel,
        out_shape=jax.ShapeDtypeStruct((144, 1024), jnp.bfloat16),
        compiler_params=pltpu.CompilerParams(vmem_limit_bytes=BIG),
        cost_estimate=CHEAP,
        name="prepare",
    )(hidden, scale)


def rotate_kernel(core_ref, w_ref, r2_ref, dv_ref, rot_ref, top_ref, keep_ref, send_ref):
    step = pl.program_id(0)
    core = core_ref[0]
    rot = jnp.dot(w_ref[...], r2_ref[...], preferred_element_type=jnp.float32).astype(jnp.bfloat16)
    rot_ref[...] = rot
    top = jnp.max(jnp.abs(rot.astype(jnp.float32)), axis=0, keepdims=True)

    @pl.when(step == 0)
    def _():
        top_ref[...] = top

    @pl.when(step > 0)
    def _():
        top_ref[...] = jnp.maximum(top_ref[...], top)

    @pl.when(step < 2)
    def _():
        for part in range(4):
            prod = dot_nt(dv_ref[...], rot[part * 512 : (part + 1) * 512]).astype(jnp.bfloat16)
            chip = step * 2 + part // 2

            @pl.when(core == part % 2)
            def _():
                keep_ref[chip] = prod

            @pl.when(core != part % 2)
            def _():
                send_ref[chip] = prod


def rotate(core, weight, rotor, value_grad):
    whole = lambda i, core: (0, 0)
    block = lambda i, core: (i, 0)
    half = jax.ShapeDtypeStruct((4, 128, 512), jnp.bfloat16)
    return pl.pallas_call(
        rotate_kernel,
        grid_spec=pltpu.PrefetchScalarGridSpec(
            num_scalar_prefetch=1,
            grid=(4,),
            in_specs=[
                pl.BlockSpec((2048, 128), block),
                pl.BlockSpec((128, 128), whole),
                pl.BlockSpec((128, 128), whole),
            ],
            out_specs=[
                pl.BlockSpec((2048, 128), block),
                pl.BlockSpec((1, 128), whole),
                pl.BlockSpec((4, 128, 512), lambda i, core: (0, 0, 0)),
                pl.BlockSpec((4, 128, 512), lambda i, core: (0, 0, 0)),
            ],
        ),
        out_shape=[
            jax.ShapeDtypeStruct((8192, 128), jnp.bfloat16),
            jax.ShapeDtypeStruct((1, 128), jnp.float32),
            half,
            half,
        ],
        compiler_params=pltpu.CompilerParams(vmem_limit_bytes=BIG),
        cost_estimate=LONG,
        name="rotate",
    )(core, weight, rotor, value_grad)


def weight_grad_kernel(rot_ref, top_ref, dv_ref, out_ref):
    step = top_ref[...] / 7.0 + SCALE_FLOOR
    quant = soft_quant(rot_ref[...].astype(jnp.float32), 1.0 / step, step * 7.0)
    out_ref[0] = dot_nt(dv_ref[...], quant.astype(jnp.bfloat16)).astype(jnp.bfloat16)


def weight_grad(rot, top, value_grad):
    return pl.pallas_call(
        weight_grad_kernel,
        grid=(8,),
        in_specs=[
            pl.BlockSpec((1024, 128), lambda i: (i, 0)),
            pl.BlockSpec((1, 128), lambda i: (0, 0)),
            pl.BlockSpec((128, 128), lambda i: (0, 0)),
        ],
        out_specs=pl.BlockSpec((1, 128, 1024), lambda i: (i, 0, 0)),
        out_shape=jax.ShapeDtypeStruct((8, 128, 1024), jnp.bfloat16),
        compiler_params=pltpu.CompilerParams(vmem_limit_bytes=BIG),
        cost_estimate=CHEAP,
        name="weight_grad",
    )(rot, top, value_grad)


def quant_kernel(half_ref, all_ref, sum_ref, mask_ref, quant_ref, inv_ref):
    squares = jnp.sum(sum_ref[...].astype(jnp.float32), axis=0)
    squares = squares[3:4] + squares[4:5] + squares[5:6]
    inverse = lax.rsqrt(squares / 8192.0 + NORM_EPS)
    inv_ref[...] = inverse
    inverse = jnp.transpose(jnp.broadcast_to(inverse, (128, 128)))
    mask = mask_ref[0]
    scale = all_ref[0, 128:144, :].astype(jnp.float32)
    scale = scale[0:1] + scale[1:2] + scale[2:3]
    recip = 1.0 / scale
    scale7 = scale * 7.0
    for lane in range(8):
        cols = slice(lane * 128, (lane + 1) * 128)
        normed = all_ref[0, 0:128, cols].astype(jnp.float32) * inverse
        soft = soft_quant(normed, recip[:, cols], scale7[:, cols])
        quant = jnp.where(mask[:, cols] > 0.0, normed, soft).astype(jnp.bfloat16)
        zh, zl, yh = lane // 4, (lane // 2) % 2, lane % 2
        place = zh * 2 + yh
        quant_ref[zl, :, place * 128 : (place + 1) * 128] = quant


def quantize(half, hidden_all, mask, name):
    return pl.pallas_call(
        quant_kernel,
        grid_spec=pltpu.PrefetchScalarGridSpec(
            num_scalar_prefetch=1,
            grid=(4,),
            in_specs=[
                pl.BlockSpec((1, 144, 1024), lambda i, half: (i * 2 + half[0], 0, 0)),
                pl.BlockSpec((8, 16, 128), lambda i, half: (0, 8, 0)),
                pl.BlockSpec((1, 1, 1024), lambda i, half: (i * 2 + half[0], 0, 0)),
            ],
            out_specs=[
                pl.BlockSpec((2, 128, 512), lambda i, half: (i, 0, 0)),
                pl.BlockSpec((1, 128), lambda i, half: (0, 0)),
            ],
        ),
        out_shape=[
            jax.ShapeDtypeStruct((8, 128, 512), jnp.bfloat16),
            jax.ShapeDtypeStruct((1, 128), jnp.float32),
        ],
        compiler_params=pltpu.CompilerParams(vmem_limit_bytes=BIG),
        cost_estimate=CHEAP,
        name=name,
    )(half, hidden_all, hidden_all, mask)


def rotor_grad_kernel(core_ref, mine_ref, other_ref, wm_ref, wo_ref, dv_ref, r2_ref, total_ref):
    step = pl.program_id(0)
    total = jnp.zeros((128, 128), jnp.float32)
    for quant_ref, weight_ref in ((mine_ref, wm_ref), (other_ref, wo_ref)):
        for lane in range(8):
            zh, zl, yh = lane // 4, (lane // 2) % 2, lane % 2
            place = zh * 2 + yh
            total += jnp.dot(
                quant_ref[zl, :, place * 128 : (place + 1) * 128],
                weight_ref[0, lane * 128 : (lane + 1) * 128, :],
                preferred_element_type=jnp.float32,
            )

    @pl.when(step == 0)
    def _():
        total_ref[...] = total

    @pl.when(step > 0)
    def _():
        total_ref[...] += total

    @pl.when(step == 3)
    def _():
        r2_ref[...] = lax.dot_general(
            total_ref[...],
            dv_ref[...].astype(jnp.float32),
            (((0,), (0,)), ((), ())),
            precision=lax.Precision.HIGHEST,
            preferred_element_type=jnp.float32,
        )


def rotor_grad(core, mine, other, weight, value_grad):
    weight = weight.reshape(8, 1024, 128)
    quant_spec = pl.BlockSpec((2, 128, 512), lambda i, core: (i, 0, 0))
    return pl.pallas_call(
        rotor_grad_kernel,
        grid_spec=pltpu.PrefetchScalarGridSpec(
            num_scalar_prefetch=1,
            grid=(4,),
            in_specs=[
                quant_spec,
                quant_spec,
                pl.BlockSpec((1, 1024, 128), lambda i, core: (i * 2 + core[0], 0, 0)),
                pl.BlockSpec((1, 1024, 128), lambda i, core: (i * 2 + 1 - core[0], 0, 0)),
                pl.BlockSpec((128, 128), lambda i, core: (0, 0)),
            ],
            out_specs=pl.BlockSpec((128, 128), lambda i, core: (0, 0)),
            scratch_shapes=[pltpu.VMEM((128, 128), jnp.float32)],
        ),
        out_shape=jax.ShapeDtypeStruct((128, 128), jnp.float32),
        compiler_params=pltpu.CompilerParams(vmem_limit_bytes=BIG),
        cost_estimate=CHEAP,
        name="rotor_grad",
    )(core, mine, other, weight, weight, value_grad)


def outer_kernel(place_ref, frame_ref, quant_ref, *rest):
    out_ref, yh = rest[-1], place_ref[1]
    prod = lax.dot_general(
        frame_ref[...],
        quant_ref[...],
        (((0,), (0,)), ((), ())),
        preferred_element_type=jnp.float32,
    ).astype(jnp.bfloat16)
    for part in range(2):
        out_ref[(part + yh) % 2] = prod[:, part * 128 : (part + 1) * 128]


def outer(place, frames, quants, into, name):
    more = [] if into is None else [into]
    return pl.pallas_call(
        outer_kernel,
        grid_spec=pltpu.PrefetchScalarGridSpec(
            num_scalar_prefetch=1,
            grid=(2,),
            in_specs=[
                pl.BlockSpec((1024, 512), lambda i, place: (0, 0)),
                pl.BlockSpec((1024, 256), lambda i, place: (0, i)),
            ]
            + [pl.BlockSpec(memory_space=pl.ANY)] * len(more),
            out_specs=pl.BlockSpec((2, 512, 128), lambda i, place: (place[0] * 2 + i, 0, 0)),
        ),
        out_shape=jax.ShapeDtypeStruct((8, 512, 128), jnp.bfloat16),
        input_output_aliases={3: 0} if more else {},
        compiler_params=pltpu.CompilerParams(vmem_limit_bytes=BIG),
        cost_estimate=CHEAP,
        name=name,
    )(place, frames, quants, *more)


def exchange(value, axes):
    return lax.all_to_all(value, axes, split_axis=0, concat_axis=0, tiled=True)


def shifted(value, axis, turn):
    count = lax.axis_size(axis)
    return lax.ppermute(value, axis, [(chip, (chip + turn) % count) for chip in range(count)])


def swap_core(value):
    return shifted(value, "c", 1)


def local(hidden_in, grad_sent, value_grad, value_weight, rotation, act_scale, outliers):
    sections = 64
    pairs = [(source, (source - 1) % sections) for source in range(sections)]
    core, yh = lax.axis_index("c"), lax.axis_index("yh")
    place = jnp.stack([core, yh]).astype(jnp.int32)
    other = jnp.stack([1 - core, yh]).astype(jnp.int32)
    wide = lambda value: value.astype(jnp.float32)
    tie = lax.optimization_barrier

    hidden_all = lax.all_gather(prepare(hidden_in, act_scale), TPA, axis=0)

    rot, peak, frame_keep, frame_send = rotate(place, value_weight, rotation, value_grad)
    frame_pair = (wide(frame_keep) + wide(swap_core(frame_send))).astype(jnp.bfloat16)
    rot, frame_pair = tie((rot, frame_pair))
    frame_terms = exchange(frame_pair, "yl")
    grad_parts = weight_grad(rot, peak, value_grad)
    frame_terms, grad_parts = tie((frame_terms, grad_parts))
    frame = jnp.sum(wide(frame_terms), axis=0).astype(jnp.bfloat16)
    frames = exchange(jnp.broadcast_to(frame[None], (8, 128, 512)), NEAR).reshape(1024, 512)

    ids = outliers[0]
    blocks = (ids[None, :] // 128 == jnp.arange(64)[:, None]).astype(jnp.bfloat16)
    lanes = (ids[:, None] % 128 == jnp.arange(128)[None, :]).astype(jnp.bfloat16)
    mask = jnp.dot(blocks, lanes, preferred_element_type=jnp.float32).reshape(TP, 1, 1024)

    hidden_all, mask, grad_parts = tie((hidden_all, mask, grad_parts))
    grad_sum = lax.psum_scatter(grad_parts, TPA, scatter_dimension=0, tiled=False)
    quant, inverse = quantize(place, hidden_all, mask, "quantize")
    frames, quant, hidden_all = tie((frames, quant, hidden_all))
    quants = exchange(quant, NEAR)
    quant_other, _ = quantize(other, hidden_all, mask, "quantize_other")
    r2_grad = rotor_grad(place, quant, quant_other, value_weight, value_grad)
    quants, r2_grad, grad_sent = tie((quants, r2_grad, grad_sent))
    quants_other = swap_core(quants).reshape(1024, 512)
    incoming = lax.ppermute(grad_sent, SEC, pairs)
    parts = outer(place, frames, quants.reshape(1024, 512), None, "outer")
    parts = outer(other, frames, quants_other, parts, "outer_other")
    parts = exchange(parts, "zh").reshape(4, 2, 512, 128)
    sums = jnp.sum(wide(parts), axis=0)
    r1_grad = sums[0] + wide(shifted(sums[1].astype(jnp.bfloat16), "yh", 1))

    mask_mine = lax.dynamic_index_in_dim(mask, lax.axis_index(TPA), 0, keepdims=False)
    inverse = inverse.reshape(128, 1)
    normed = wide(hidden_in) * inverse
    bounded = jnp.tanh(normed / (7.0 * act_scale))
    slope = jnp.where(mask_mine > 0.0, 1.0, 1.0 - bounded * bounded)
    emitted = (wide(incoming) + inverse * (wide(grad_sum) * slope)).astype(jnp.bfloat16)
    return (emitted, r1_grad, r2_grad)


def solution(mesh):
    fine = Mesh(mesh.devices.reshape(4, 4, 2, 2, 4, 2), SEC + TPA)
    both = P(SEC, TPA)
    in_specs = (both, both, both, both, both, both, P(SEC, None))
    out_specs = (both, P(TPA, SEC), both)
    return jax.shard_map(local, mesh=fine, in_specs=in_specs, out_specs=out_specs, check_vma=False)
```

```python
import math

import jax
import jax.numpy as jnp
from jax import lax
from jax.experimental import pallas as pl
from jax.experimental.pallas import tpu as pltpu
from jax.sharding import Mesh
from jax.sharding import PartitionSpec as P

ROWS_OUT = 4096
NORM_EPS = 1e-05
SCALE_FLOOR = 1e-06
TP = 8
BIG = 32 << 20
CHEAP = pl.CostEstimate(flops=1, bytes_accessed=1, transcendentals=0)
LONG = pl.CostEstimate(flops=23_000_000_000, bytes_accessed=1, transcendentals=0)
SEC = ("x", "zh", "zl", "yh")
TPA = ("yl", "c")
NEAR = ("x", "zl")
FAR = ("zh", "yh")
SIN_POLY = (
    0.9999995827674866,
    -6.579691410064697,
    12.986435890197754,
    -12.188101768493652,
    6.558041572570801,
    -1.9530311822891235,
)


def soft_quant(values, inv_step, step7):
    scaled = values * inv_step
    turn = scaled - jnp.round(scaled)
    square = turn * turn
    poly = SIN_POLY[-1]
    for coef in SIN_POLY[-2::-1]:
        poly = poly * square + coef
    shifted = scaled - turn * poly
    return step7 * jnp.tanh(shifted * (1.0 / 7.0))


def dot_nt(left, right):
    return lax.dot_general(
        left, right, (((1,), (1,)), ((), ())), preferred_element_type=jnp.float32
    )


def prepare_kernel(x_ref, scale_ref, out_ref):
    scale = scale_ref[...]
    top = scale.astype(jnp.bfloat16).astype(jnp.float32)
    rest = scale - top
    mid = rest.astype(jnp.bfloat16).astype(jnp.float32)
    low = rest - mid
    row = lax.broadcasted_iota(jnp.int32, (16, scale.shape[1]), 0)
    extra = jnp.where(row == 0, top, jnp.where(row == 1, mid, jnp.where(row == 2, low, 0.0)))
    out_ref[0:128, :] = x_ref[...]
    out_ref[128:144, :] = extra.astype(jnp.bfloat16)


def prepare(hidden, scale):
    return pl.pallas_call(
        prepare_kernel,
        out_shape=jax.ShapeDtypeStruct((144, 1024), jnp.bfloat16),
        compiler_params=pltpu.CompilerParams(vmem_limit_bytes=BIG),
        cost_estimate=CHEAP,
        name="prepare",
    )(hidden, scale)


def rotated_rows(w_ref, r2_ref):
    rot = jnp.dot(w_ref[...], r2_ref[...], preferred_element_type=jnp.float32)
    return rot.astype(jnp.bfloat16)


def keep_top(top_ref, rot):
    step = pl.program_id(0)
    top = jnp.max(jnp.abs(rot.astype(jnp.float32)), axis=0, keepdims=True)

    @pl.when(step == 0)
    def _():
        top_ref[...] = top

    @pl.when(step > 0)
    def _():
        top_ref[...] = jnp.maximum(top_ref[...], top)


def frame_kernel(core_ref, w_ref, r2_ref, dv_ref, top_ref, keep_ref, send_ref):
    core = core_ref[0]
    rot = rotated_rows(w_ref, r2_ref)
    keep_top(top_ref, rot)
    for part in range(4):
        prod = dot_nt(dv_ref[...], rot[part * 512 : (part + 1) * 512]).astype(jnp.bfloat16)

        @pl.when(core == part % 2)
        def _():
            keep_ref[part // 2] = prod

        @pl.when(core != part % 2)
        def _():
            send_ref[part // 2] = prod


def frame_parts(core, weight, rotor, value_grad):
    whole = lambda i, core: (0, 0)
    half = jax.ShapeDtypeStruct((4, 128, 512), jnp.bfloat16)
    return pl.pallas_call(
        frame_kernel,
        grid_spec=pltpu.PrefetchScalarGridSpec(
            num_scalar_prefetch=1,
            grid=(2,),
            in_specs=[
                pl.BlockSpec((2048, 128), lambda i, core: (i, 0)),
                pl.BlockSpec((128, 128), whole),
                pl.BlockSpec((128, 128), whole),
            ],
            out_specs=[
                pl.BlockSpec((1, 128), whole),
                pl.BlockSpec((2, 128, 512), lambda i, core: (i, 0, 0)),
                pl.BlockSpec((2, 128, 512), lambda i, core: (i, 0, 0)),
            ],
        ),
        out_shape=[jax.ShapeDtypeStruct((1, 128), jnp.float32), half, half],
        compiler_params=pltpu.CompilerParams(vmem_limit_bytes=BIG),
        cost_estimate=LONG,
        name="frame_parts",
    )(core, weight, rotor, value_grad)


def top_kernel(w_ref, r2_ref, top_ref):
    keep_top(top_ref, rotated_rows(w_ref, r2_ref))


def rest_top(weight, rotor):
    return pl.pallas_call(
        top_kernel,
        grid=(2,),
        in_specs=[
            pl.BlockSpec((2048, 128), lambda i: (i + 2, 0)),
            pl.BlockSpec((128, 128), lambda i: (0, 0)),
        ],
        out_specs=pl.BlockSpec((1, 128), lambda i: (0, 0)),
        out_shape=jax.ShapeDtypeStruct((1, 128), jnp.float32),
        compiler_params=pltpu.CompilerParams(vmem_limit_bytes=BIG),
        cost_estimate=CHEAP,
        name="rest_top",
    )(weight, rotor)


def weight_grad_kernel(w_ref, r2_ref, one_ref, two_ref, dv_ref, out_ref):
    step = jnp.maximum(one_ref[...], two_ref[...]) / 7.0 + SCALE_FLOOR
    rot = rotated_rows(w_ref, r2_ref).astype(jnp.float32)
    quant = soft_quant(rot, 1.0 / step, step * 7.0)
    out_ref[0] = dot_nt(dv_ref[...], quant.astype(jnp.bfloat16)).astype(jnp.bfloat16)


def weight_grad(weight, rotor, top_one, top_two, value_grad):
    small = pl.BlockSpec((128, 128), lambda i: (0, 0))
    row = pl.BlockSpec((1, 128), lambda i: (0, 0))
    return pl.pallas_call(
        weight_grad_kernel,
        grid=(8,),
        in_specs=[pl.BlockSpec((1024, 128), lambda i: (i, 0)), small, row, row, small],
        out_specs=pl.BlockSpec((1, 128, 1024), lambda i: (i, 0, 0)),
        out_shape=jax.ShapeDtypeStruct((8, 128, 1024), jnp.bfloat16),
        compiler_params=pltpu.CompilerParams(vmem_limit_bytes=BIG),
        cost_estimate=CHEAP,
        name="weight_grad",
    )(weight, rotor, top_one, top_two, value_grad)


def quant_kernel(core_ref, all_ref, mask_ref, inv_ref, quant_ref):
    inverse = jnp.transpose(jnp.broadcast_to(inv_ref[...], (128, 128)))
    mask = mask_ref[0]
    scale = all_ref[0, 128:144, :].astype(jnp.float32)
    scale = scale[0:1] + scale[1:2] + scale[2:3]
    recip = 1.0 / scale
    scale7 = scale * 7.0
    for lane in range(8):
        cols = slice(lane * 128, (lane + 1) * 128)
        normed = all_ref[0, 0:128, cols].astype(jnp.float32) * inverse
        soft = soft_quant(normed, recip[:, cols], scale7[:, cols])
        quant = jnp.where(mask[:, cols] > 0.0, normed, soft).astype(jnp.bfloat16)
        zh, zl, yh = lane // 4, (lane // 2) % 2, lane % 2
        place = zh * 2 + yh
        quant_ref[zl, :, place * 128 : (place + 1) * 128] = quant


def quantize(core, hidden_all, mask, inverse):
    return pl.pallas_call(
        quant_kernel,
        grid_spec=pltpu.PrefetchScalarGridSpec(
            num_scalar_prefetch=1,
            grid=(4,),
            in_specs=[
                pl.BlockSpec((1, 144, 1024), lambda i, core: (i, 0, 0)),
                pl.BlockSpec((1, 1, 1024), lambda i, core: (i * 2 + core[0], 0, 0)),
                pl.BlockSpec((1, 128), lambda i, core: (0, 0)),
            ],
            out_specs=pl.BlockSpec((2, 128, 512), lambda i, core: (i, 0, 0)),
        ),
        out_shape=jax.ShapeDtypeStruct((8, 128, 512), jnp.bfloat16),
        compiler_params=pltpu.CompilerParams(vmem_limit_bytes=BIG),
        cost_estimate=pl.CostEstimate(flops=10_350_000_000, bytes_accessed=1, transcendentals=0),
        name="quantize",
    )(core, hidden_all, mask, inverse)


def rotor_grad_kernel(core_ref, mine_ref, other_ref, wm_ref, wo_ref, dv_ref, r2_ref, total_ref):
    step = pl.program_id(0)
    total = jnp.zeros((128, 128), jnp.float32)
    for quant_ref, weight_ref in ((mine_ref, wm_ref), (other_ref, wo_ref)):
        for lane in range(8):
            zh, zl, yh = lane // 4, (lane // 2) % 2, lane % 2
            place = zh * 2 + yh
            total += jnp.dot(
                quant_ref[zl, :, place * 128 : (place + 1) * 128],
                weight_ref[0, lane * 128 : (lane + 1) * 128, :],
                preferred_element_type=jnp.float32,
            )

    @pl.when(step == 0)
    def _():
        total_ref[...] = total

    @pl.when(step > 0)
    def _():
        total_ref[...] += total

    @pl.when(step == 3)
    def _():
        r2_ref[...] = lax.dot_general(
            total_ref[...],
            dv_ref[...].astype(jnp.float32),
            (((0,), (0,)), ((), ())),
            precision=lax.Precision.HIGHEST,
            preferred_element_type=jnp.float32,
        )


def rotor_grad(core, mine, other, weight, value_grad):
    weight = weight.reshape(8, 1024, 128)
    quant_spec = pl.BlockSpec((2, 128, 512), lambda i, core: (i, 0, 0))
    return pl.pallas_call(
        rotor_grad_kernel,
        grid_spec=pltpu.PrefetchScalarGridSpec(
            num_scalar_prefetch=1,
            grid=(4,),
            in_specs=[
                quant_spec,
                quant_spec,
                pl.BlockSpec((1, 1024, 128), lambda i, core: (i * 2 + core[0], 0, 0)),
                pl.BlockSpec((1, 1024, 128), lambda i, core: (i * 2 + 1 - core[0], 0, 0)),
                pl.BlockSpec((128, 128), lambda i, core: (0, 0)),
            ],
            out_specs=pl.BlockSpec((128, 128), lambda i, core: (0, 0)),
            scratch_shapes=[pltpu.VMEM((128, 128), jnp.float32)],
        ),
        out_shape=jax.ShapeDtypeStruct((128, 128), jnp.float32),
        compiler_params=pltpu.CompilerParams(vmem_limit_bytes=BIG),
        cost_estimate=CHEAP,
        name="rotor_grad",
    )(core, mine, other, weight, weight, value_grad)


def outer_kernel(place_ref, frame_ref, quant_ref, *rest):
    out_ref, yh = rest[-1], place_ref[1]
    prod = lax.dot_general(
        frame_ref[...],
        quant_ref[...],
        (((0,), (0,)), ((), ())),
        preferred_element_type=jnp.float32,
    ).astype(jnp.bfloat16)
    for part in range(2):
        out_ref[(part + yh) % 2] = prod[:, part * 128 : (part + 1) * 128]


def outer(place, frames, quants, into, name):
    more = [] if into is None else [into]
    return pl.pallas_call(
        outer_kernel,
        grid_spec=pltpu.PrefetchScalarGridSpec(
            num_scalar_prefetch=1,
            grid=(2,),
            in_specs=[
                pl.BlockSpec((1024, 512), lambda i, place: (0, 0)),
                pl.BlockSpec((1024, 256), lambda i, place: (0, i)),
            ]
            + [pl.BlockSpec(memory_space=pl.ANY)] * len(more),
            out_specs=pl.BlockSpec((2, 512, 128), lambda i, place: (place[0] * 2 + i, 0, 0)),
        ),
        out_shape=jax.ShapeDtypeStruct((8, 512, 128), jnp.bfloat16),
        input_output_aliases={3: 0} if more else {},
        compiler_params=pltpu.CompilerParams(vmem_limit_bytes=BIG),
        cost_estimate=CHEAP,
        name=name,
    )(place, frames, quants, *more)


def exchange(value, axes):
    return lax.all_to_all(value, axes, split_axis=0, concat_axis=0, tiled=True)


def shifted(value, axis, turn):
    count = lax.axis_size(axis)
    return lax.ppermute(value, axis, [(chip, (chip + turn) % count) for chip in range(count)])


def swap_core(value):
    return shifted(value, "c", 1)


def flipped(value, bit):
    return lax.ppermute(value, "yl", [(chip, chip ^ bit) for chip in range(4)])


def local(hidden_in, grad_sent, value_grad, value_weight, rotation, act_scale, outliers):
    sections = 64
    pairs = [(source, (source - 1) % sections) for source in range(sections)]
    core, yh = lax.axis_index("c"), lax.axis_index("yh")
    place = jnp.stack([core, yh]).astype(jnp.int32)
    other = jnp.stack([1 - core, yh]).astype(jnp.int32)
    wide = lambda value: value.astype(jnp.float32)
    tie = lax.optimization_barrier

    hidden_all = lax.all_gather(prepare(hidden_in, act_scale), "yl", axis=0)

    top_one, frame_keep, frame_send = frame_parts(place, value_weight, rotation, value_grad)
    frame_pair = (wide(frame_keep) + wide(swap_core(frame_send))).astype(jnp.bfloat16)
    frame_pair, hidden_two = tie((frame_pair, hidden_in))
    frame_terms = exchange(frame_pair, "yl")
    squares = jnp.sum(wide(hidden_two) * wide(hidden_two), axis=1).reshape(1, 128)
    squares = squares + swap_core(squares)
    squares = squares + flipped(squares, 1)
    squares = squares + flipped(squares, 2)
    inverse = lax.rsqrt(squares / 8192.0 + NORM_EPS)
    frame_terms, inverse, rotor = tie((frame_terms, inverse, rotation))
    frame = jnp.sum(wide(frame_terms), axis=0).astype(jnp.bfloat16)
    frames = exchange(jnp.broadcast_to(frame[None], (8, 128, 512)), NEAR).reshape(1024, 512)
    top_two = rest_top(value_weight, rotor)
    grad_parts = weight_grad(value_weight, rotor, top_one, top_two, value_grad)

    ids = outliers[0]
    blocks = (ids[None, :] // 128 == jnp.arange(64)[:, None]).astype(jnp.bfloat16)
    lanes = (ids[:, None] % 128 == jnp.arange(128)[None, :]).astype(jnp.bfloat16)
    mask = jnp.dot(blocks, lanes, preferred_element_type=jnp.float32).reshape(TP, 1, 1024)

    hidden_all, mask, grad_parts = tie((hidden_all, mask, grad_parts))
    grad_sum = lax.psum_scatter(grad_parts, TPA, scatter_dimension=0, tiled=False)
    quant = quantize(place, hidden_all, mask, inverse)
    frames, quant = tie((frames, quant))
    quants = exchange(quant, NEAR)
    r2_grad = rotor_grad(place, quant, swap_core(quant), value_weight, value_grad)
    quants, r2_grad, grad_sent = tie((quants, r2_grad, grad_sent))
    quants_other = swap_core(quants).reshape(1024, 512)
    incoming = lax.ppermute(grad_sent, SEC, pairs)
    parts = outer(place, frames, quants.reshape(1024, 512), None, "outer")
    parts = outer(other, frames, quants_other, parts, "outer_other")
    parts = exchange(parts, "zh").reshape(4, 2, 512, 128)
    sums = jnp.sum(wide(parts), axis=0)
    r1_grad = sums[0] + wide(shifted(sums[1].astype(jnp.bfloat16), "yh", 1))

    mask_mine = lax.dynamic_index_in_dim(mask, lax.axis_index(TPA), 0, keepdims=False)
    inverse = inverse.reshape(128, 1)
    normed = wide(hidden_in) * inverse
    bounded = jnp.tanh(normed / (7.0 * act_scale))
    slope = jnp.where(mask_mine > 0.0, 1.0, 1.0 - bounded * bounded)
    emitted = (wide(incoming) + inverse * (wide(grad_sum) * slope)).astype(jnp.bfloat16)
    return (emitted, r1_grad, r2_grad)


def solution(mesh):
    fine = Mesh(mesh.devices.reshape(4, 4, 2, 2, 4, 2), SEC + TPA)
    both = P(SEC, TPA)
    in_specs = (both, both, both, both, both, both, P(SEC, None))
    out_specs = (both, P(TPA, SEC), both)
    return jax.shard_map(local, mesh=fine, in_specs=in_specs, out_specs=out_specs, check_vma=False)
```

```python
import math

import jax
import jax.numpy as jnp
from jax import lax
from jax.experimental import pallas as pl
from jax.experimental.pallas import tpu as pltpu
from jax.sharding import Mesh
from jax.sharding import PartitionSpec as P

ROWS_OUT = 4096
NORM_EPS = 1e-05
SCALE_FLOOR = 1e-06
TP = 8
BIG = 32 << 20
CHEAP = pl.CostEstimate(flops=1, bytes_accessed=1, transcendentals=0)
LONG = pl.CostEstimate(flops=23_000_000_000, bytes_accessed=1, transcendentals=0)
SEC = ("x", "zh", "zl", "yh")
TPA = ("yl", "c")
NEAR = ("x", "zl")
FAR = ("zh", "yh")
SIN_POLY = (
    0.9999995827674866,
    -6.579691410064697,
    12.986435890197754,
    -12.188101768493652,
    6.558041572570801,
    -1.9530311822891235,
)


def soft_quant(values, inv_step, step7):
    scaled = values * inv_step
    turn = scaled - jnp.round(scaled)
    square = turn * turn
    poly = SIN_POLY[-1]
    for coef in SIN_POLY[-2::-1]:
        poly = poly * square + coef
    shifted = scaled - turn * poly
    return step7 * jnp.tanh(shifted * (1.0 / 7.0))


def dot_nt(left, right):
    return lax.dot_general(
        left, right, (((1,), (1,)), ((), ())), preferred_element_type=jnp.float32
    )


def prepare_kernel(x_ref, scale_ref, out_ref):
    scale = scale_ref[...]
    top = scale.astype(jnp.bfloat16).astype(jnp.float32)
    rest = scale - top
    mid = rest.astype(jnp.bfloat16).astype(jnp.float32)
    low = rest - mid
    row = lax.broadcasted_iota(jnp.int32, (16, scale.shape[1]), 0)
    extra = jnp.where(row == 0, top, jnp.where(row == 1, mid, jnp.where(row == 2, low, 0.0)))
    out_ref[0:128, :] = x_ref[...]
    out_ref[128:144, :] = extra.astype(jnp.bfloat16)


def prepare(hidden, scale):
    return pl.pallas_call(
        prepare_kernel,
        out_shape=jax.ShapeDtypeStruct((144, 1024), jnp.bfloat16),
        compiler_params=pltpu.CompilerParams(vmem_limit_bytes=BIG),
        cost_estimate=CHEAP,
        name="prepare",
    )(hidden, scale)


def rotated_rows(w_ref, r2_ref):
    rot = jnp.dot(w_ref[...], r2_ref[...], preferred_element_type=jnp.float32)
    return rot.astype(jnp.bfloat16)


def keep_top(top_ref, rot):
    step = pl.program_id(0)
    top = jnp.max(jnp.abs(rot.astype(jnp.float32)), axis=0, keepdims=True)

    @pl.when(step == 0)
    def _():
        top_ref[...] = top

    @pl.when(step > 0)
    def _():
        top_ref[...] = jnp.maximum(top_ref[...], top)


def frame_kernel(core_ref, w_ref, r2_ref, dv_ref, top_ref, keep_ref, send_ref):
    core = core_ref[0]
    rot = rotated_rows(w_ref, r2_ref)
    keep_top(top_ref, rot)
    for part in range(4):
        prod = dot_nt(rot[part * 512 : (part + 1) * 512], dv_ref[...]).astype(jnp.bfloat16)

        @pl.when(core == part % 2)
        def _():
            keep_ref[part // 2] = prod

        @pl.when(core != part % 2)
        def _():
            send_ref[part // 2] = prod


def frame_parts(core, weight, rotor, value_grad):
    whole = lambda i, core: (0, 0)
    half = jax.ShapeDtypeStruct((4, 512, 128), jnp.bfloat16)
    return pl.pallas_call(
        frame_kernel,
        grid_spec=pltpu.PrefetchScalarGridSpec(
            num_scalar_prefetch=1,
            grid=(2,),
            in_specs=[
                pl.BlockSpec((2048, 128), lambda i, core: (i, 0)),
                pl.BlockSpec((128, 128), whole),
                pl.BlockSpec((128, 128), whole),
            ],
            out_specs=[
                pl.BlockSpec((1, 128), whole),
                pl.BlockSpec((2, 512, 128), lambda i, core: (i, 0, 0)),
                pl.BlockSpec((2, 512, 128), lambda i, core: (i, 0, 0)),
            ],
        ),
        out_shape=[jax.ShapeDtypeStruct((1, 128), jnp.float32), half, half],
        compiler_params=pltpu.CompilerParams(vmem_limit_bytes=BIG),
        cost_estimate=LONG,
        name="frame_parts",
    )(core, weight, rotor, value_grad)


def top_kernel(w_ref, r2_ref, top_ref):
    keep_top(top_ref, rotated_rows(w_ref, r2_ref))


def rest_top(weight, rotor):
    return pl.pallas_call(
        top_kernel,
        grid=(2,),
        in_specs=[
            pl.BlockSpec((2048, 128), lambda i: (i + 2, 0)),
            pl.BlockSpec((128, 128), lambda i: (0, 0)),
        ],
        out_specs=pl.BlockSpec((1, 128), lambda i: (0, 0)),
        out_shape=jax.ShapeDtypeStruct((1, 128), jnp.float32),
        compiler_params=pltpu.CompilerParams(vmem_limit_bytes=BIG),
        cost_estimate=CHEAP,
        name="rest_top",
    )(weight, rotor)


def weight_grad_kernel(w_ref, r2_ref, one_ref, two_ref, dv_ref, out_ref):
    step = jnp.maximum(one_ref[...], two_ref[...]) / 7.0 + SCALE_FLOOR
    rot = rotated_rows(w_ref, r2_ref).astype(jnp.float32)
    quant = soft_quant(rot, 1.0 / step, step * 7.0)
    out_ref[0] = dot_nt(dv_ref[...], quant.astype(jnp.bfloat16)).astype(jnp.bfloat16)


def weight_grad(weight, rotor, top_one, top_two, value_grad):
    small = pl.BlockSpec((128, 128), lambda i: (0, 0))
    row = pl.BlockSpec((1, 128), lambda i: (0, 0))
    return pl.pallas_call(
        weight_grad_kernel,
        grid=(8,),
        in_specs=[pl.BlockSpec((1024, 128), lambda i: (i, 0)), small, row, row, small],
        out_specs=pl.BlockSpec((1, 128, 1024), lambda i: (i, 0, 0)),
        out_shape=jax.ShapeDtypeStruct((8, 128, 1024), jnp.bfloat16),
        compiler_params=pltpu.CompilerParams(vmem_limit_bytes=BIG),
        cost_estimate=pl.CostEstimate(flops=10_350_000_000, bytes_accessed=1, transcendentals=0),
        name="weight_grad",
    )(weight, rotor, top_one, top_two, value_grad)


def quant_kernel(core_ref, all_ref, mask_ref, inv_ref, quant_ref):
    inverse = jnp.transpose(jnp.broadcast_to(inv_ref[...], (128, 128)))
    mask = mask_ref[0]
    scale = all_ref[0, 128:144, :].astype(jnp.float32)
    scale = scale[0:1] + scale[1:2] + scale[2:3]
    recip = 1.0 / scale
    scale7 = scale * 7.0
    for lane in range(8):
        cols = slice(lane * 128, (lane + 1) * 128)
        normed = all_ref[0, 0:128, cols].astype(jnp.float32) * inverse
        soft = soft_quant(normed, recip[:, cols], scale7[:, cols])
        quant = jnp.where(mask[:, cols] > 0.0, normed, soft).astype(jnp.bfloat16)
        zh, zl, yh = lane // 4, (lane // 2) % 2, lane % 2
        place = zh * 2 + yh
        quant_ref[zl, :, place * 128 : (place + 1) * 128] = quant


def quantize(core, hidden_all, mask, inverse):
    return pl.pallas_call(
        quant_kernel,
        grid_spec=pltpu.PrefetchScalarGridSpec(
            num_scalar_prefetch=1,
            grid=(4,),
            in_specs=[
                pl.BlockSpec((1, 144, 1024), lambda i, core: (i, 0, 0)),
                pl.BlockSpec((1, 1, 1024), lambda i, core: (i * 2 + core[0], 0, 0)),
                pl.BlockSpec((1, 128), lambda i, core: (0, 0)),
            ],
            out_specs=pl.BlockSpec((2, 128, 512), lambda i, core: (i, 0, 0)),
        ),
        out_shape=jax.ShapeDtypeStruct((8, 128, 512), jnp.bfloat16),
        compiler_params=pltpu.CompilerParams(vmem_limit_bytes=BIG),
        cost_estimate=pl.CostEstimate(flops=6_900_000_000, bytes_accessed=1, transcendentals=0),
        name="quantize",
    )(core, hidden_all, mask, inverse)


def rotor_grad_kernel(core_ref, mine_ref, other_ref, wm_ref, wo_ref, dv_ref, r2_ref, total_ref):
    step = pl.program_id(0)
    total = jnp.zeros((128, 128), jnp.float32)
    for quant_ref, weight_ref in ((mine_ref, wm_ref), (other_ref, wo_ref)):
        for lane in range(8):
            zh, zl, yh = lane // 4, (lane // 2) % 2, lane % 2
            place = zh * 2 + yh
            total += jnp.dot(
                quant_ref[zl, :, place * 128 : (place + 1) * 128],
                weight_ref[0, lane * 128 : (lane + 1) * 128, :],
                preferred_element_type=jnp.float32,
            )

    @pl.when(step == 0)
    def _():
        total_ref[...] = total

    @pl.when(step > 0)
    def _():
        total_ref[...] += total

    @pl.when(step == 3)
    def _():
        r2_ref[...] = lax.dot_general(
            total_ref[...],
            dv_ref[...].astype(jnp.float32),
            (((0,), (0,)), ((), ())),
            precision=lax.Precision.HIGHEST,
            preferred_element_type=jnp.float32,
        )


def rotor_grad(core, mine, other, weight, value_grad):
    weight = weight.reshape(8, 1024, 128)
    quant_spec = pl.BlockSpec((2, 128, 512), lambda i, core: (i, 0, 0))
    return pl.pallas_call(
        rotor_grad_kernel,
        grid_spec=pltpu.PrefetchScalarGridSpec(
            num_scalar_prefetch=1,
            grid=(4,),
            in_specs=[
                quant_spec,
                quant_spec,
                pl.BlockSpec((1, 1024, 128), lambda i, core: (i * 2 + core[0], 0, 0)),
                pl.BlockSpec((1, 1024, 128), lambda i, core: (i * 2 + 1 - core[0], 0, 0)),
                pl.BlockSpec((128, 128), lambda i, core: (0, 0)),
            ],
            out_specs=pl.BlockSpec((128, 128), lambda i, core: (0, 0)),
            scratch_shapes=[pltpu.VMEM((128, 128), jnp.float32)],
        ),
        out_shape=jax.ShapeDtypeStruct((128, 128), jnp.float32),
        compiler_params=pltpu.CompilerParams(vmem_limit_bytes=BIG),
        cost_estimate=CHEAP,
        name="rotor_grad",
    )(core, mine, other, weight, weight, value_grad)


def outer_kernel(place_ref, frame_ref, quant_ref, *rest):
    out_ref, left_ref, yh = rest[-2], rest[-1], place_ref[1]

    @pl.when(pl.program_id(0) == 0)
    def _():
        for near in range(8):
            left_ref[:, near * 128 : (near + 1) * 128] = frame_ref[near]

    prod = jnp.dot(left_ref[...], quant_ref[...], preferred_element_type=jnp.float32)
    prod = prod.astype(jnp.bfloat16)
    for part in range(2):
        out_ref[(part + yh) % 2] = prod[:, part * 128 : (part + 1) * 128]


def outer(place, frames, quants, into, name):
    more = [] if into is None else [into]
    return pl.pallas_call(
        outer_kernel,
        grid_spec=pltpu.PrefetchScalarGridSpec(
            num_scalar_prefetch=1,
            grid=(2,),
            in_specs=[
                pl.BlockSpec((8, 512, 128), lambda i, place: (0, 0, 0)),
                pl.BlockSpec((1024, 256), lambda i, place: (0, i)),
            ]
            + [pl.BlockSpec(memory_space=pl.ANY)] * len(more),
            out_specs=pl.BlockSpec((2, 512, 128), lambda i, place: (place[0] * 2 + i, 0, 0)),
            scratch_shapes=[pltpu.VMEM((512, 1024), jnp.bfloat16)],
        ),
        out_shape=jax.ShapeDtypeStruct((8, 512, 128), jnp.bfloat16),
        input_output_aliases={3: 0} if more else {},
        compiler_params=pltpu.CompilerParams(vmem_limit_bytes=BIG),
        cost_estimate=CHEAP,
        name=name,
    )(place, frames, quants, *more)


def exchange(value, axes):
    return lax.all_to_all(value, axes, split_axis=0, concat_axis=0, tiled=True)


def shifted(value, axis, turn):
    count = lax.axis_size(axis)
    return lax.ppermute(value, axis, [(chip, (chip + turn) % count) for chip in range(count)])


def swap_core(value):
    return shifted(value, "c", 1)


def flipped(value, bit):
    return lax.ppermute(value, "yl", [(chip, chip ^ bit) for chip in range(4)])


def local(hidden_in, grad_sent, value_grad, value_weight, rotation, act_scale, outliers):
    sections = 64
    pairs = [(source, (source - 1) % sections) for source in range(sections)]
    core, yh = lax.axis_index("c"), lax.axis_index("yh")
    place = jnp.stack([core, yh]).astype(jnp.int32)
    other = jnp.stack([1 - core, yh]).astype(jnp.int32)
    wide = lambda value: value.astype(jnp.float32)
    tie = lax.optimization_barrier

    hidden_all = lax.all_gather(prepare(hidden_in, act_scale), "yl", axis=0)

    top_one, frame_keep, frame_send = frame_parts(place, value_weight, rotation, value_grad)
    frame_pair = (wide(frame_keep) + wide(swap_core(frame_send))).astype(jnp.bfloat16)
    frame_pair, rotor = tie((frame_pair, rotation))
    frame_terms = exchange(frame_pair, "yl")
    top_two = rest_top(value_weight, rotor)
    grad_parts = weight_grad(value_weight, rotor, top_one, top_two, value_grad)
    frame_terms, grad_parts, hidden_two = tie((frame_terms, grad_parts, hidden_in))
    frame = jnp.sum(wide(frame_terms), axis=0).astype(jnp.bfloat16)
    frames = exchange(jnp.broadcast_to(frame[None], (8, 512, 128)), NEAR)
    squares = jnp.sum(wide(hidden_two) * wide(hidden_two), axis=1).reshape(1, 128)
    squares = squares + swap_core(squares)
    squares = squares + flipped(squares, 1)
    squares = squares + flipped(squares, 2)
    inverse = lax.rsqrt(squares / 8192.0 + NORM_EPS)

    ids = outliers[0]
    blocks = (ids[None, :] // 128 == jnp.arange(64)[:, None]).astype(jnp.bfloat16)
    lanes = (ids[:, None] % 128 == jnp.arange(128)[None, :]).astype(jnp.bfloat16)
    mask = jnp.dot(blocks, lanes, preferred_element_type=jnp.float32).reshape(TP, 1, 1024)

    hidden_all, mask, grad_parts, inverse = tie((hidden_all, mask, grad_parts, inverse))
    grad_sum = lax.psum_scatter(grad_parts, TPA, scatter_dimension=0, tiled=False)
    quant = quantize(place, hidden_all, mask, inverse)
    frames, quant = tie((frames, quant))
    quants = exchange(quant, NEAR)
    quants, quant, grad_sent = tie((quants, quant, grad_sent))
    quants_other = swap_core(quants).reshape(1024, 512)
    incoming = lax.ppermute(grad_sent, SEC, pairs)
    parts = outer(place, frames, quants.reshape(1024, 512), None, "outer")
    parts = outer(other, frames, quants_other, parts, "outer_other")
    r2_grad = rotor_grad(place, quant, swap_core(quant), value_weight, value_grad)
    parts, r2_grad = tie((exchange(parts, "zh").reshape(4, 2, 512, 128), r2_grad))
    sums = jnp.sum(wide(parts), axis=0)
    r1_grad = sums[0] + wide(shifted(sums[1].astype(jnp.bfloat16), "yh", 1))

    mask_mine = lax.dynamic_index_in_dim(mask, lax.axis_index(TPA), 0, keepdims=False)
    inverse = inverse.reshape(128, 1)
    normed = wide(hidden_in) * inverse
    bounded = jnp.tanh(normed / (7.0 * act_scale))
    slope = jnp.where(mask_mine > 0.0, 1.0, 1.0 - bounded * bounded)
    emitted = (wide(incoming) + inverse * (wide(grad_sum) * slope)).astype(jnp.bfloat16)
    return (emitted, r1_grad, r2_grad)


def solution(mesh):
    fine = Mesh(mesh.devices.reshape(4, 4, 2, 2, 4, 2), SEC + TPA)
    both = P(SEC, TPA)
    in_specs = (both, both, both, both, both, both, P(SEC, None))
    out_specs = (both, P(TPA, SEC), both)
    return jax.shard_map(local, mesh=fine, in_specs=in_specs, out_specs=out_specs, check_vma=False)
```

```python
import math

import jax
import jax.numpy as jnp
from jax import lax
from jax.experimental import pallas as pl
from jax.experimental.pallas import tpu as pltpu
from jax.sharding import Mesh
from jax.sharding import PartitionSpec as P

ROWS_OUT = 4096
NORM_EPS = 1e-05
SCALE_FLOOR = 1e-06
TP = 8
BIG = 32 << 20
WHOLE = 60 << 20
CHEAP = pl.CostEstimate(flops=1, bytes_accessed=1, transcendentals=0)
LONG = pl.CostEstimate(flops=23_000_000_000, bytes_accessed=1, transcendentals=0)
SEC = ("x", "zh", "zl", "yh")
TPA = ("yl", "c")
NEAR = ("x", "zl")
FAR = ("zh", "yh")
SIN_POLY = (
    0.9999995827674866,
    -6.579691410064697,
    12.986435890197754,
    -12.188101768493652,
    6.558041572570801,
    -1.9530311822891235,
)


def soft_quant(values, inv_step, step7):
    scaled = values * inv_step
    turn = scaled - jnp.round(scaled)
    square = turn * turn
    poly = SIN_POLY[-1]
    for coef in SIN_POLY[-2::-1]:
        poly = poly * square + coef
    shifted = scaled - turn * poly
    return step7 * jnp.tanh(shifted * (1.0 / 7.0))


def dot_nt(left, right):
    return lax.dot_general(
        left, right, (((1,), (1,)), ((), ())), preferred_element_type=jnp.float32
    )


def prepare_kernel(core_ref, x_ref, scale_ref, w_ref, r2_ref, dv_ref, out_ref, send_ref):
    step = pl.program_id(0)
    send_ref[pl.ds(pl.multiple_of(step * 512, 512), 512), :] = w_ref[...]

    @pl.when(step == 0)
    def _():
        scale = scale_ref[...]
        top = scale.astype(jnp.bfloat16).astype(jnp.float32)
        rest = scale - top
        mid = rest.astype(jnp.bfloat16).astype(jnp.float32)
        low = rest - mid
        row = lax.broadcasted_iota(jnp.int32, (16, scale.shape[1]), 0)
        extra = jnp.where(row == 0, top, jnp.where(row == 1, mid, jnp.where(row == 2, low, 0.0)))
        out_ref[0:128, :] = x_ref[...]
        out_ref[128:144, :] = extra.astype(jnp.bfloat16)
        send_ref[2048:2176, :] = r2_ref[...]
        send_ref[2176:2304, :] = dv_ref[...]


def prepare(core, hidden, scale, weight, rotor, value_grad):
    whole = lambda i, core: (0, 0)
    return pl.pallas_call(
        prepare_kernel,
        grid_spec=pltpu.PrefetchScalarGridSpec(
            num_scalar_prefetch=1,
            grid=(4,),
            in_specs=[
                pl.BlockSpec((128, 1024), whole),
                pl.BlockSpec((1, 1024), whole),
                pl.BlockSpec((512, 128), lambda i, core: (i * 2 + 1 - core[0], 0)),
                pl.BlockSpec((128, 128), whole),
                pl.BlockSpec((128, 128), whole),
            ],
            out_specs=[pl.BlockSpec((144, 1024), whole), pl.BlockSpec((2304, 128), whole)],
        ),
        out_shape=[
            jax.ShapeDtypeStruct((144, 1024), jnp.bfloat16),
            jax.ShapeDtypeStruct((2304, 128), jnp.bfloat16),
        ],
        compiler_params=pltpu.CompilerParams(vmem_limit_bytes=WHOLE),
        cost_estimate=CHEAP,
        name="prepare",
    )(core, hidden, scale, weight, rotor, value_grad)


def rotated_rows(w_ref, r2_ref):
    rot = jnp.dot(w_ref[...], r2_ref[...], preferred_element_type=jnp.float32)
    return rot.astype(jnp.bfloat16)


def keep_top(top_ref, rot):
    step = pl.program_id(0)
    top = jnp.max(jnp.abs(rot.astype(jnp.float32)), axis=0, keepdims=True)

    @pl.when(step == 0)
    def _():
        top_ref[...] = top

    @pl.when(step > 0)
    def _():
        top_ref[...] = jnp.maximum(top_ref[...], top)


def frame_kernel(core_ref, w_ref, r2_ref, dv_ref, w2_ref, r22_ref, dv2_ref, out_ref):
    mine = dot_nt(dv_ref[...], rotated_rows(w_ref, r2_ref))
    other = dot_nt(dv2_ref[...], rotated_rows(w2_ref, r22_ref))
    out_ref[0] = (mine + other).astype(jnp.bfloat16)


def frame_pairs(core, weight, rotor, value_grad, received):
    whole = pl.BlockSpec((128, 128), lambda i, core: (0, 0))
    return pl.pallas_call(
        frame_kernel,
        grid_spec=pltpu.PrefetchScalarGridSpec(
            num_scalar_prefetch=1,
            grid=(4,),
            in_specs=[
                pl.BlockSpec((512, 128), lambda i, core: (i * 2 + core[0], 0)),
                whole,
                whole,
                pl.BlockSpec((512, 128), lambda i, core: (i, 0)),
                pl.BlockSpec((128, 128), lambda i, core: (16, 0)),
                pl.BlockSpec((128, 128), lambda i, core: (17, 0)),
            ],
            out_specs=pl.BlockSpec((1, 128, 512), lambda i, core: (i, 0, 0)),
        ),
        out_shape=jax.ShapeDtypeStruct((4, 128, 512), jnp.bfloat16),
        compiler_params=pltpu.CompilerParams(vmem_limit_bytes=BIG),
        cost_estimate=LONG,
        name="frame_pairs",
    )(core, weight, rotor, value_grad, received, received, received)


def top_kernel(w_ref, r2_ref, top_ref):
    keep_top(top_ref, rotated_rows(w_ref, r2_ref))


def rotated_top(weight, rotor):
    return pl.pallas_call(
        top_kernel,
        grid=(4,),
        in_specs=[
            pl.BlockSpec((2048, 128), lambda i: (i, 0)),
            pl.BlockSpec((128, 128), lambda i: (0, 0)),
        ],
        out_specs=pl.BlockSpec((1, 128), lambda i: (0, 0)),
        out_shape=jax.ShapeDtypeStruct((1, 128), jnp.float32),
        compiler_params=pltpu.CompilerParams(vmem_limit_bytes=BIG),
        cost_estimate=CHEAP,
        name="rotated_top",
    )(weight, rotor)


def weight_grad_kernel(w_ref, r2_ref, top_ref, dv_ref, out_ref):
    step = top_ref[...] / 7.0 + SCALE_FLOOR
    rot = rotated_rows(w_ref, r2_ref).astype(jnp.float32)
    quant = soft_quant(rot, 1.0 / step, step * 7.0)
    out_ref[0] = dot_nt(dv_ref[...], quant.astype(jnp.bfloat16)).astype(jnp.bfloat16)


def weight_grad(weight, rotor, top, value_grad):
    small = pl.BlockSpec((128, 128), lambda i: (0, 0))
    row = pl.BlockSpec((1, 128), lambda i: (0, 0))
    return pl.pallas_call(
        weight_grad_kernel,
        grid=(8,),
        in_specs=[pl.BlockSpec((1024, 128), lambda i: (i, 0)), small, row, small],
        out_specs=pl.BlockSpec((1, 128, 1024), lambda i: (i, 0, 0)),
        out_shape=jax.ShapeDtypeStruct((8, 128, 1024), jnp.bfloat16),
        compiler_params=pltpu.CompilerParams(vmem_limit_bytes=BIG),
        cost_estimate=CHEAP,
        name="weight_grad",
    )(weight, rotor, top, value_grad)


def quant_kernel(core_ref, all_ref, mask_ref, inv_ref, quant_ref):
    inverse = jnp.transpose(jnp.broadcast_to(inv_ref[...], (128, 128)))
    mask = mask_ref[0]
    scale = all_ref[0, 128:144, :].astype(jnp.float32)
    scale = scale[0:1] + scale[1:2] + scale[2:3]
    recip = 1.0 / scale
    scale7 = scale * 7.0
    for lane in range(8):
        cols = slice(lane * 128, (lane + 1) * 128)
        normed = all_ref[0, 0:128, cols].astype(jnp.float32) * inverse
        soft = soft_quant(normed, recip[:, cols], scale7[:, cols])
        quant = jnp.where(mask[:, cols] > 0.0, normed, soft).astype(jnp.bfloat16)
        zh, zl, yh = lane // 4, (lane // 2) % 2, lane % 2
        place = zh * 2 + yh
        quant_ref[zl, :, place * 128 : (place + 1) * 128] = quant


def quantize(core, hidden_all, mask, inverse):
    return pl.pallas_call(
        quant_kernel,
        grid_spec=pltpu.PrefetchScalarGridSpec(
            num_scalar_prefetch=1,
            grid=(4,),
            in_specs=[
                pl.BlockSpec((1, 144, 1024), lambda i, core: (i, 0, 0)),
                pl.BlockSpec((1, 1, 1024), lambda i, core: (i * 2 + core[0], 0, 0)),
                pl.BlockSpec((1, 128), lambda i, core: (0, 0)),
            ],
            out_specs=pl.BlockSpec((2, 128, 512), lambda i, core: (i, 0, 0)),
        ),
        out_shape=jax.ShapeDtypeStruct((8, 128, 512), jnp.bfloat16),
        compiler_params=pltpu.CompilerParams(vmem_limit_bytes=BIG),
        cost_estimate=pl.CostEstimate(flops=10_350_000_000, bytes_accessed=1, transcendentals=0),
        name="quantize",
    )(core, hidden_all, mask, inverse)


def rotor_grad_kernel(core_ref, mine_ref, other_ref, wm_ref, wo_ref, dv_ref, r2_ref, total_ref):
    step = pl.program_id(0)
    total = jnp.zeros((128, 128), jnp.float32)
    for quant_ref, weight_ref in ((mine_ref, wm_ref), (other_ref, wo_ref)):
        for lane in range(8):
            zh, zl, yh = lane // 4, (lane // 2) % 2, lane % 2
            place = zh * 2 + yh
            total += jnp.dot(
                quant_ref[zl, :, place * 128 : (place + 1) * 128],
                weight_ref[0, lane * 128 : (lane + 1) * 128, :],
                preferred_element_type=jnp.float32,
            )

    @pl.when(step == 0)
    def _():
        total_ref[...] = total

    @pl.when(step > 0)
    def _():
        total_ref[...] += total

    @pl.when(step == 3)
    def _():
        r2_ref[...] = lax.dot_general(
            total_ref[...],
            dv_ref[...].astype(jnp.float32),
            (((0,), (0,)), ((), ())),
            precision=lax.Precision.HIGHEST,
            preferred_element_type=jnp.float32,
        )


def rotor_grad(core, mine, other, weight, value_grad):
    weight = weight.reshape(8, 1024, 128)
    quant_spec = pl.BlockSpec((2, 128, 512), lambda i, core: (i, 0, 0))
    return pl.pallas_call(
        rotor_grad_kernel,
        grid_spec=pltpu.PrefetchScalarGridSpec(
            num_scalar_prefetch=1,
            grid=(4,),
            in_specs=[
                quant_spec,
                quant_spec,
                pl.BlockSpec((1, 1024, 128), lambda i, core: (i * 2 + core[0], 0, 0)),
                pl.BlockSpec((1, 1024, 128), lambda i, core: (i * 2 + 1 - core[0], 0, 0)),
                pl.BlockSpec((128, 128), lambda i, core: (0, 0)),
            ],
            out_specs=pl.BlockSpec((128, 128), lambda i, core: (0, 0)),
            scratch_shapes=[pltpu.VMEM((128, 128), jnp.float32)],
        ),
        out_shape=jax.ShapeDtypeStruct((128, 128), jnp.float32),
        compiler_params=pltpu.CompilerParams(vmem_limit_bytes=BIG),
        cost_estimate=CHEAP,
        name="rotor_grad",
    )(core, mine, other, weight, weight, value_grad)


def outer_kernel(place_ref, frame_ref, quant_ref, *rest):
    out_ref, yh = rest[-1], place_ref[1]
    prod = lax.dot_general(
        frame_ref[...],
        quant_ref[...],
        (((0,), (0,)), ((), ())),
        preferred_element_type=jnp.float32,
    ).astype(jnp.bfloat16)
    for part in range(2):
        out_ref[(part + yh) % 2] = prod[:, part * 128 : (part + 1) * 128]


def outer(place, frames, quants, into, name):
    more = [] if into is None else [into]
    return pl.pallas_call(
        outer_kernel,
        grid_spec=pltpu.PrefetchScalarGridSpec(
            num_scalar_prefetch=1,
            grid=(2,),
            in_specs=[
                pl.BlockSpec((1024, 512), lambda i, place: (0, 0)),
                pl.BlockSpec((1024, 256), lambda i, place: (0, i)),
            ]
            + [pl.BlockSpec(memory_space=pl.ANY)] * len(more),
            out_specs=pl.BlockSpec((2, 512, 128), lambda i, place: (place[0] * 2 + i, 0, 0)),
        ),
        out_shape=jax.ShapeDtypeStruct((8, 512, 128), jnp.bfloat16),
        input_output_aliases={3: 0} if more else {},
        compiler_params=pltpu.CompilerParams(vmem_limit_bytes=BIG),
        cost_estimate=CHEAP,
        name=name,
    )(place, frames, quants, *more)


def exchange(value, axes):
    return lax.all_to_all(value, axes, split_axis=0, concat_axis=0, tiled=True)


def shifted(value, axis, turn):
    count = lax.axis_size(axis)
    return lax.ppermute(value, axis, [(chip, (chip + turn) % count) for chip in range(count)])


def swap_core(value):
    return shifted(value, "c", 1)


def flipped(value, bit):
    return lax.ppermute(value, "yl", [(chip, chip ^ bit) for chip in range(4)])


def local(hidden_in, grad_sent, value_grad, value_weight, rotation, act_scale, outliers):
    sections = 64
    pairs = [(source, (source - 1) % sections) for source in range(sections)]
    core, yh = lax.axis_index("c"), lax.axis_index("yh")
    place = jnp.stack([core, yh]).astype(jnp.int32)
    other = jnp.stack([1 - core, yh]).astype(jnp.int32)
    wide = lambda value: value.astype(jnp.float32)
    tie = lax.optimization_barrier

    packed, inputs = prepare(place, hidden_in, act_scale, value_weight, rotation, value_grad)
    hidden_all = lax.all_gather(packed, "yl", axis=0)

    frame_pair = frame_pairs(place, value_weight, rotation, value_grad, swap_core(inputs))
    frame_pair, hidden_two = tie((frame_pair, hidden_in))
    frame_terms = exchange(frame_pair, "yl")
    squares = jnp.sum(wide(hidden_two) * wide(hidden_two), axis=1).reshape(1, 128)
    squares = squares + swap_core(squares)
    squares = squares + flipped(squares, 1)
    squares = squares + flipped(squares, 2)
    inverse = lax.rsqrt(squares / 8192.0 + NORM_EPS)
    frame_terms, inverse, rotor = tie((frame_terms, inverse, rotation))
    frame = jnp.sum(wide(frame_terms), axis=0).astype(jnp.bfloat16)
    frames = exchange(jnp.broadcast_to(frame[None], (8, 128, 512)), NEAR).reshape(1024, 512)
    top = rotated_top(value_weight, rotor)
    grad_parts = weight_grad(value_weight, rotor, top, value_grad)

    ids = outliers[0]
    blocks = (ids[None, :] // 128 == jnp.arange(64)[:, None]).astype(jnp.bfloat16)
    lanes = (ids[:, None] % 128 == jnp.arange(128)[None, :]).astype(jnp.bfloat16)
    mask = jnp.dot(blocks, lanes, preferred_element_type=jnp.float32).reshape(TP, 1, 1024)

    hidden_all, mask, grad_parts = tie((hidden_all, mask, grad_parts))
    grad_sum = lax.psum_scatter(grad_parts, TPA, scatter_dimension=0, tiled=False)
    quant = quantize(place, hidden_all, mask, inverse)
    frames, quant = tie((frames, quant))
    quants = exchange(quant, NEAR)
    quants, quant, grad_sent = tie((quants, quant, grad_sent))
    quants_other = swap_core(quants).reshape(1024, 512)
    incoming = lax.ppermute(grad_sent, SEC, pairs)
    parts = outer(place, frames, quants.reshape(1024, 512), None, "outer")
    parts = outer(other, frames, quants_other, parts, "outer_other")
    r2_grad = rotor_grad(place, quant, swap_core(quant), value_weight, value_grad)
    parts, r2_grad = tie((exchange(parts, "zh").reshape(4, 2, 512, 128), r2_grad))
    sums = jnp.sum(wide(parts), axis=0)
    r1_grad = sums[0] + wide(shifted(sums[1].astype(jnp.bfloat16), "yh", 1))

    mask_mine = lax.dynamic_index_in_dim(mask, lax.axis_index(TPA), 0, keepdims=False)
    inverse = inverse.reshape(128, 1)
    normed = wide(hidden_in) * inverse
    bounded = jnp.tanh(normed / (7.0 * act_scale))
    slope = jnp.where(mask_mine > 0.0, 1.0, 1.0 - bounded * bounded)
    emitted = (wide(incoming) + inverse * (wide(grad_sum) * slope)).astype(jnp.bfloat16)
    return (emitted, r1_grad, r2_grad)


def solution(mesh):
    fine = Mesh(mesh.devices.reshape(4, 4, 2, 2, 4, 2), SEC + TPA)
    both = P(SEC, TPA)
    in_specs = (both, both, both, both, both, both, P(SEC, None))
    out_specs = (both, P(TPA, SEC), both)
    return jax.shard_map(local, mesh=fine, in_specs=in_specs, out_specs=out_specs, check_vma=False)
```

```python
import math

import jax
import jax.numpy as jnp
from jax import lax
from jax.experimental import pallas as pl
from jax.experimental.pallas import tpu as pltpu
from jax.sharding import Mesh
from jax.sharding import PartitionSpec as P

ROWS_OUT = 4096
NORM_EPS = 1e-05
SCALE_FLOOR = 1e-06
TP = 8
BIG = 32 << 20
WHOLE = 60 << 20
CHEAP = pl.CostEstimate(flops=1, bytes_accessed=1, transcendentals=0)
LONG = pl.CostEstimate(flops=23_000_000_000, bytes_accessed=1, transcendentals=0)
SEC = ("x", "zh", "zl", "yh")
TPA = ("yl", "c")
NEAR = ("x", "zl")
FAR = ("zh", "yh")
SIN_POLY = (
    0.9999995827674866,
    -6.579691410064697,
    12.986435890197754,
    -12.188101768493652,
    6.558041572570801,
    -1.9530311822891235,
)


def soft_quant(values, inv_step, step7):
    scaled = values * inv_step
    turn = scaled - jnp.round(scaled)
    square = turn * turn
    poly = SIN_POLY[-1]
    for coef in SIN_POLY[-2::-1]:
        poly = poly * square + coef
    shifted = scaled - turn * poly
    return step7 * jnp.tanh(shifted * (1.0 / 7.0))


def dot_nt(left, right):
    return lax.dot_general(
        left, right, (((1,), (1,)), ((), ())), preferred_element_type=jnp.float32
    )


def three_terms(value):
    top = value.astype(jnp.bfloat16).astype(jnp.float32)
    rest = value - top
    mid = rest.astype(jnp.bfloat16).astype(jnp.float32)
    return top, mid, rest - mid


def in_rows(terms, width):
    row = lax.broadcasted_iota(jnp.int32, (16, width), 0)
    out = jnp.zeros((16, width), jnp.float32)
    for index, term in enumerate(terms):
        out = jnp.where(row == index, term, out)
    return out.astype(jnp.bfloat16)


def inputs_kernel(core_ref, x_ref, w_ref, r2_ref, dv_ref, send_ref):
    step = pl.program_id(0)
    send_ref[pl.ds(pl.multiple_of(step * 512, 512), 512), :] = w_ref[...]

    @pl.when(step == 0)
    def _():
        squares = jnp.zeros((128, 128), jnp.float32)
        for lane in range(8):
            x = x_ref[:, lane * 128 : (lane + 1) * 128].astype(jnp.float32)
            squares += x * x
        squares = jnp.sum(jnp.transpose(squares), axis=0, keepdims=True)
        send_ref[2048:2176, :] = r2_ref[...]
        send_ref[2176:2304, :] = dv_ref[...]
        send_ref[2304:2320, :] = in_rows(three_terms(squares), 128)


def core_inputs(core, hidden, weight, rotor, value_grad):
    whole = lambda i, core: (0, 0)
    return pl.pallas_call(
        inputs_kernel,
        grid_spec=pltpu.PrefetchScalarGridSpec(
            num_scalar_prefetch=1,
            grid=(4,),
            in_specs=[
                pl.BlockSpec((128, 1024), whole),
                pl.BlockSpec((512, 128), lambda i, core: (i * 2 + 1 - core[0], 0)),
                pl.BlockSpec((128, 128), whole),
                pl.BlockSpec((128, 128), whole),
            ],
            out_specs=pl.BlockSpec((2320, 128), whole),
        ),
        out_shape=jax.ShapeDtypeStruct((2320, 128), jnp.bfloat16),
        compiler_params=pltpu.CompilerParams(vmem_limit_bytes=WHOLE),
        cost_estimate=CHEAP,
        name="core_inputs",
    )(core, hidden, weight, rotor, value_grad)


def pack_kernel(x_ref, scale_ref, mine_ref, other_ref, out_ref):
    terms = mine_ref[...].astype(jnp.float32), other_ref[...].astype(jnp.float32)
    sums = [term[0:1] + term[1:2] + term[2:3] for term in terms]
    squares = jnp.concatenate([sums[0] + sums[1], jnp.zeros((1, 896), jnp.float32)], axis=1)
    out_ref[0:128, :] = x_ref[...]
    out_ref[128:144, :] = in_rows(three_terms(scale_ref[...]) + three_terms(squares), 1024)


def pack(hidden, scale, mine, other):
    whole = lambda i: (0, 0)
    return pl.pallas_call(
        pack_kernel,
        grid=(1,),
        in_specs=[
            pl.BlockSpec((128, 1024), whole),
            pl.BlockSpec((1, 1024), whole),
            pl.BlockSpec((16, 128), lambda i: (144, 0)),
            pl.BlockSpec((16, 128), lambda i: (144, 0)),
        ],
        out_specs=pl.BlockSpec((144, 1024), whole),
        out_shape=jax.ShapeDtypeStruct((144, 1024), jnp.bfloat16),
        compiler_params=pltpu.CompilerParams(vmem_limit_bytes=BIG),
        cost_estimate=CHEAP,
        name="pack",
    )(hidden, scale, mine, other)


def rotated_rows(w_ref, r2_ref):
    rot = jnp.dot(w_ref[...], r2_ref[...], preferred_element_type=jnp.float32)
    return rot.astype(jnp.bfloat16)


def keep_top(top_ref, rot):
    step = pl.program_id(0)
    top = jnp.max(jnp.abs(rot.astype(jnp.float32)), axis=0, keepdims=True)

    @pl.when(step == 0)
    def _():
        top_ref[...] = top

    @pl.when(step > 0)
    def _():
        top_ref[...] = jnp.maximum(top_ref[...], top)


def frame_kernel(core_ref, w_ref, r2_ref, dv_ref, w2_ref, r22_ref, dv2_ref, out_ref):
    mine = dot_nt(dv_ref[...], rotated_rows(w_ref, r2_ref))
    other = dot_nt(dv2_ref[...], rotated_rows(w2_ref, r22_ref))
    out_ref[0] = (mine + other).astype(jnp.bfloat16)


def frame_pairs(core, weight, rotor, value_grad, received):
    whole = pl.BlockSpec((128, 128), lambda i, core: (0, 0))
    return pl.pallas_call(
        frame_kernel,
        grid_spec=pltpu.PrefetchScalarGridSpec(
            num_scalar_prefetch=1,
            grid=(4,),
            in_specs=[
                pl.BlockSpec((512, 128), lambda i, core: (i * 2 + core[0], 0)),
                whole,
                whole,
                pl.BlockSpec((512, 128), lambda i, core: (i, 0)),
                pl.BlockSpec((128, 128), lambda i, core: (16, 0)),
                pl.BlockSpec((128, 128), lambda i, core: (17, 0)),
            ],
            out_specs=pl.BlockSpec((1, 128, 512), lambda i, core: (i, 0, 0)),
        ),
        out_shape=jax.ShapeDtypeStruct((4, 128, 512), jnp.bfloat16),
        compiler_params=pltpu.CompilerParams(vmem_limit_bytes=BIG),
        cost_estimate=LONG,
        name="frame_pairs",
    )(core, weight, rotor, value_grad, received, received, received)


def top_kernel(w_ref, r2_ref, top_ref):
    keep_top(top_ref, rotated_rows(w_ref, r2_ref))


def rotated_top(weight, rotor):
    return pl.pallas_call(
        top_kernel,
        grid=(4,),
        in_specs=[
            pl.BlockSpec((2048, 128), lambda i: (i, 0)),
            pl.BlockSpec((128, 128), lambda i: (0, 0)),
        ],
        out_specs=pl.BlockSpec((1, 128), lambda i: (0, 0)),
        out_shape=jax.ShapeDtypeStruct((1, 128), jnp.float32),
        compiler_params=pltpu.CompilerParams(vmem_limit_bytes=BIG),
        cost_estimate=CHEAP,
        name="rotated_top",
    )(weight, rotor)


def weight_grad_kernel(w_ref, r2_ref, top_ref, dv_ref, out_ref):
    step = top_ref[...] / 7.0 + SCALE_FLOOR
    rot = rotated_rows(w_ref, r2_ref).astype(jnp.float32)
    quant = soft_quant(rot, 1.0 / step, step * 7.0)
    out_ref[0] = dot_nt(dv_ref[...], quant.astype(jnp.bfloat16)).astype(jnp.bfloat16)


def weight_grad(weight, rotor, top, value_grad):
    small = pl.BlockSpec((128, 128), lambda i: (0, 0))
    row = pl.BlockSpec((1, 128), lambda i: (0, 0))
    return pl.pallas_call(
        weight_grad_kernel,
        grid=(8,),
        in_specs=[pl.BlockSpec((1024, 128), lambda i: (i, 0)), small, row, small],
        out_specs=pl.BlockSpec((1, 128, 1024), lambda i: (i, 0, 0)),
        out_shape=jax.ShapeDtypeStruct((8, 128, 1024), jnp.bfloat16),
        compiler_params=pltpu.CompilerParams(vmem_limit_bytes=BIG),
        cost_estimate=CHEAP,
        name="weight_grad",
    )(weight, rotor, top, value_grad)


def quant_kernel(core_ref, all_ref, sum_ref, mask_ref, quant_ref, inv_ref):
    squares = jnp.sum(sum_ref[...].astype(jnp.float32), axis=0)
    squares = squares[3:4] + squares[4:5] + squares[5:6]
    inverse = lax.rsqrt(squares / 8192.0 + NORM_EPS)
    inv_ref[...] = inverse
    inverse = jnp.transpose(jnp.broadcast_to(inverse, (128, 128)))
    mask = mask_ref[0]
    scale = all_ref[0, 128:144, :].astype(jnp.float32)
    scale = scale[0:1] + scale[1:2] + scale[2:3]
    recip = 1.0 / scale
    scale7 = scale * 7.0
    for lane in range(8):
        cols = slice(lane * 128, (lane + 1) * 128)
        normed = all_ref[0, 0:128, cols].astype(jnp.float32) * inverse
        soft = soft_quant(normed, recip[:, cols], scale7[:, cols])
        quant = jnp.where(mask[:, cols] > 0.0, normed, soft).astype(jnp.bfloat16)
        zh, zl, yh = lane // 4, (lane // 2) % 2, lane % 2
        place = zh * 2 + yh
        quant_ref[zl, :, place * 128 : (place + 1) * 128] = quant


def quantize(core, hidden_all, mask):
    return pl.pallas_call(
        quant_kernel,
        grid_spec=pltpu.PrefetchScalarGridSpec(
            num_scalar_prefetch=1,
            grid=(4,),
            in_specs=[
                pl.BlockSpec((1, 144, 1024), lambda i, core: (i, 0, 0)),
                pl.BlockSpec((4, 16, 128), lambda i, core: (0, 8, 0)),
                pl.BlockSpec((1, 1, 1024), lambda i, core: (i * 2 + core[0], 0, 0)),
            ],
            out_specs=[
                pl.BlockSpec((2, 128, 512), lambda i, core: (i, 0, 0)),
                pl.BlockSpec((1, 128), lambda i, core: (0, 0)),
            ],
        ),
        out_shape=[
            jax.ShapeDtypeStruct((8, 128, 512), jnp.bfloat16),
            jax.ShapeDtypeStruct((1, 128), jnp.float32),
        ],
        compiler_params=pltpu.CompilerParams(vmem_limit_bytes=BIG),
        cost_estimate=pl.CostEstimate(flops=10_350_000_000, bytes_accessed=1, transcendentals=0),
        name="quantize",
    )(core, hidden_all, hidden_all, mask)


def rotor_grad_kernel(core_ref, mine_ref, other_ref, wm_ref, wo_ref, dv_ref, r2_ref, total_ref):
    step = pl.program_id(0)
    total = jnp.zeros((128, 128), jnp.float32)
    for quant_ref, weight_ref in ((mine_ref, wm_ref), (other_ref, wo_ref)):
        for lane in range(8):
            zh, zl, yh = lane // 4, (lane // 2) % 2, lane % 2
            place = zh * 2 + yh
            total += jnp.dot(
                quant_ref[zl, :, place * 128 : (place + 1) * 128],
                weight_ref[0, lane * 128 : (lane + 1) * 128, :],
                preferred_element_type=jnp.float32,
            )

    @pl.when(step == 0)
    def _():
        total_ref[...] = total

    @pl.when(step > 0)
    def _():
        total_ref[...] += total

    @pl.when(step == 3)
    def _():
        r2_ref[...] = lax.dot_general(
            total_ref[...],
            dv_ref[...].astype(jnp.float32),
            (((0,), (0,)), ((), ())),
            precision=lax.Precision.HIGHEST,
            preferred_element_type=jnp.float32,
        )


def rotor_grad(core, mine, other, weight, value_grad):
    weight = weight.reshape(8, 1024, 128)
    quant_spec = pl.BlockSpec((2, 128, 512), lambda i, core: (i, 0, 0))
    return pl.pallas_call(
        rotor_grad_kernel,
        grid_spec=pltpu.PrefetchScalarGridSpec(
            num_scalar_prefetch=1,
            grid=(4,),
            in_specs=[
                quant_spec,
                quant_spec,
                pl.BlockSpec((1, 1024, 128), lambda i, core: (i * 2 + core[0], 0, 0)),
                pl.BlockSpec((1, 1024, 128), lambda i, core: (i * 2 + 1 - core[0], 0, 0)),
                pl.BlockSpec((128, 128), lambda i, core: (0, 0)),
            ],
            out_specs=pl.BlockSpec((128, 128), lambda i, core: (0, 0)),
            scratch_shapes=[pltpu.VMEM((128, 128), jnp.float32)],
        ),
        out_shape=jax.ShapeDtypeStruct((128, 128), jnp.float32),
        compiler_params=pltpu.CompilerParams(vmem_limit_bytes=BIG),
        cost_estimate=CHEAP,
        name="rotor_grad",
    )(core, mine, other, weight, weight, value_grad)


def outer_kernel(place_ref, frame_ref, quant_ref, *rest):
    out_ref, yh = rest[-1], place_ref[1]
    prod = lax.dot_general(
        frame_ref[...],
        quant_ref[...],
        (((0,), (0,)), ((), ())),
        preferred_element_type=jnp.float32,
    ).astype(jnp.bfloat16)
    for part in range(2):
        out_ref[(part + yh) % 2] = prod[:, part * 128 : (part + 1) * 128]


def outer(place, frames, quants, into, name):
    more = [] if into is None else [into]
    return pl.pallas_call(
        outer_kernel,
        grid_spec=pltpu.PrefetchScalarGridSpec(
            num_scalar_prefetch=1,
            grid=(2,),
            in_specs=[
                pl.BlockSpec((1024, 512), lambda i, place: (0, 0)),
                pl.BlockSpec((1024, 256), lambda i, place: (0, i)),
            ]
            + [pl.BlockSpec(memory_space=pl.ANY)] * len(more),
            out_specs=pl.BlockSpec((2, 512, 128), lambda i, place: (place[0] * 2 + i, 0, 0)),
        ),
        out_shape=jax.ShapeDtypeStruct((8, 512, 128), jnp.bfloat16),
        input_output_aliases={3: 0} if more else {},
        compiler_params=pltpu.CompilerParams(vmem_limit_bytes=BIG),
        cost_estimate=CHEAP,
        name=name,
    )(place, frames, quants, *more)


def exchange(value, axes):
    return lax.all_to_all(value, axes, split_axis=0, concat_axis=0, tiled=True)


def shifted(value, axis, turn):
    count = lax.axis_size(axis)
    return lax.ppermute(value, axis, [(chip, (chip + turn) % count) for chip in range(count)])


def swap_core(value):
    return shifted(value, "c", 1)


def local(hidden_in, grad_sent, value_grad, value_weight, rotation, act_scale, outliers):
    sections = 64
    pairs = [(source, (source - 1) % sections) for source in range(sections)]
    core, yh = lax.axis_index("c"), lax.axis_index("yh")
    place = jnp.stack([core, yh]).astype(jnp.int32)
    other = jnp.stack([1 - core, yh]).astype(jnp.int32)
    wide = lambda value: value.astype(jnp.float32)
    tie = lax.optimization_barrier

    inputs = core_inputs(place, hidden_in, value_weight, rotation, value_grad)
    received = swap_core(inputs)
    packed = pack(hidden_in, act_scale, inputs, received)
    hidden_all = lax.all_gather(packed, "yl", axis=0)

    frame_pair = frame_pairs(place, value_weight, rotation, value_grad, received)
    frame_pair, rotor = tie((frame_pair, rotation))
    frame_terms = exchange(frame_pair, "yl")
    top = rotated_top(value_weight, rotor)
    grad_parts = weight_grad(value_weight, rotor, top, value_grad)
    frame_terms, grad_parts = tie((frame_terms, grad_parts))
    frame = jnp.sum(wide(frame_terms), axis=0).astype(jnp.bfloat16)
    frames = exchange(jnp.broadcast_to(frame[None], (8, 128, 512)), NEAR).reshape(1024, 512)

    ids = outliers[0]
    blocks = (ids[None, :] // 128 == jnp.arange(64)[:, None]).astype(jnp.bfloat16)
    lanes = (ids[:, None] % 128 == jnp.arange(128)[None, :]).astype(jnp.bfloat16)
    mask = jnp.dot(blocks, lanes, preferred_element_type=jnp.float32).reshape(TP, 1, 1024)

    hidden_all, mask, grad_parts = tie((hidden_all, mask, grad_parts))
    grad_sum = lax.psum_scatter(grad_parts, TPA, scatter_dimension=0, tiled=False)
    quant, inverse = quantize(place, hidden_all, mask)
    frames, quant = tie((frames, quant))
    quants = exchange(quant, NEAR)
    quants, quant, grad_sent = tie((quants, quant, grad_sent))
    quants_other = swap_core(quants).reshape(1024, 512)
    incoming = lax.ppermute(grad_sent, SEC, pairs)
    parts = outer(place, frames, quants.reshape(1024, 512), None, "outer")
    parts = outer(other, frames, quants_other, parts, "outer_other")
    r2_grad = rotor_grad(place, quant, swap_core(quant), value_weight, value_grad)
    parts, r2_grad = tie((exchange(parts, "zh").reshape(4, 2, 512, 128), r2_grad))
    sums = jnp.sum(wide(parts), axis=0)
    r1_grad = sums[0] + wide(shifted(sums[1].astype(jnp.bfloat16), "yh", 1))

    mask_mine = lax.dynamic_index_in_dim(mask, lax.axis_index(TPA), 0, keepdims=False)
    inverse = inverse.reshape(128, 1)
    normed = wide(hidden_in) * inverse
    bounded = jnp.tanh(normed / (7.0 * act_scale))
    slope = jnp.where(mask_mine > 0.0, 1.0, 1.0 - bounded * bounded)
    emitted = (wide(incoming) + inverse * (wide(grad_sum) * slope)).astype(jnp.bfloat16)
    return (emitted, r1_grad, r2_grad)


def solution(mesh):
    fine = Mesh(mesh.devices.reshape(4, 4, 2, 2, 4, 2), SEC + TPA)
    both = P(SEC, TPA)
    in_specs = (both, both, both, both, both, both, P(SEC, None))
    out_specs = (both, P(TPA, SEC), both)
    return jax.shard_map(local, mesh=fine, in_specs=in_specs, out_specs=out_specs, check_vma=False)
```

```python
import math

import jax
import jax.numpy as jnp
from jax import lax
from jax.experimental import pallas as pl
from jax.experimental.pallas import tpu as pltpu
from jax.sharding import Mesh
from jax.sharding import PartitionSpec as P

ROWS_OUT = 4096
NORM_EPS = 1e-05
SCALE_FLOOR = 1e-06
TP = 8
BIG = 32 << 20
WHOLE = 60 << 20
CHEAP = pl.CostEstimate(flops=1, bytes_accessed=1, transcendentals=0)
LONG = pl.CostEstimate(flops=23_000_000_000, bytes_accessed=1, transcendentals=0)
SEC = ("x", "zh", "zl", "yh")
TPA = ("yl", "c")
NEAR = ("x", "zl")
FAR = ("zh", "yh")
SIN_POLY = (
    0.9999995827674866,
    -6.579691410064697,
    12.986435890197754,
    -12.188101768493652,
    6.558041572570801,
    -1.9530311822891235,
)


def soft_quant(values, inv_step, step7):
    scaled = values * inv_step
    turn = scaled - jnp.round(scaled)
    square = turn * turn
    poly = SIN_POLY[-1]
    for coef in SIN_POLY[-2::-1]:
        poly = poly * square + coef
    shifted = scaled - turn * poly
    return step7 * jnp.tanh(shifted * (1.0 / 7.0))


def dot_nt(left, right):
    return lax.dot_general(
        left, right, (((1,), (1,)), ((), ())), preferred_element_type=jnp.float32
    )


def three_terms(value):
    top = value.astype(jnp.bfloat16).astype(jnp.float32)
    rest = value - top
    mid = rest.astype(jnp.bfloat16).astype(jnp.float32)
    return top, mid, rest - mid


def in_rows(terms, width):
    row = lax.broadcasted_iota(jnp.int32, (16, width), 0)
    out = jnp.zeros((16, width), jnp.float32)
    for index, term in enumerate(terms):
        out = jnp.where(row == index, term, out)
    return out.astype(jnp.bfloat16)


def inputs_kernel(core_ref, x_ref, w_ref, r2_ref, dv_ref, send_ref):
    step = pl.program_id(0)
    send_ref[pl.ds(pl.multiple_of(step * 512, 512), 512), :] = w_ref[...]

    @pl.when(step == 0)
    def _():
        squares = jnp.zeros((128, 128), jnp.float32)
        for lane in range(8):
            x = x_ref[:, lane * 128 : (lane + 1) * 128].astype(jnp.float32)
            squares += x * x
        squares = jnp.sum(jnp.transpose(squares), axis=0, keepdims=True)
        send_ref[2048:2176, :] = r2_ref[...]
        send_ref[2176:2304, :] = dv_ref[...]
        send_ref[2304:2320, :] = in_rows(three_terms(squares), 128)


def core_inputs(core, hidden, weight, rotor, value_grad):
    whole = lambda i, core: (0, 0)
    return pl.pallas_call(
        inputs_kernel,
        grid_spec=pltpu.PrefetchScalarGridSpec(
            num_scalar_prefetch=1,
            grid=(4,),
            in_specs=[
                pl.BlockSpec((128, 1024), whole),
                pl.BlockSpec((512, 128), lambda i, core: (i * 2 + 1 - core[0], 0)),
                pl.BlockSpec((128, 128), whole),
                pl.BlockSpec((128, 128), whole),
            ],
            out_specs=pl.BlockSpec((2320, 128), whole),
        ),
        out_shape=jax.ShapeDtypeStruct((2320, 128), jnp.bfloat16),
        compiler_params=pltpu.CompilerParams(vmem_limit_bytes=WHOLE),
        cost_estimate=CHEAP,
        name="core_inputs",
    )(core, hidden, weight, rotor, value_grad)


def rotated_rows(w_ref, r2_ref):
    rot = jnp.dot(w_ref[...], r2_ref[...], preferred_element_type=jnp.float32)
    return rot.astype(jnp.bfloat16)


def keep_top(top_ref, rot):
    step = pl.program_id(0)
    top = jnp.max(jnp.abs(rot.astype(jnp.float32)), axis=0, keepdims=True)

    @pl.when(step == 0)
    def _():
        top_ref[...] = top

    @pl.when(step > 0)
    def _():
        top_ref[...] = jnp.maximum(top_ref[...], top)


def frame_kernel(
    core_ref, w_ref, r2_ref, dv_ref, w2_ref, r22_ref, dv2_ref, scale_ref, sq_ref, sq2_ref, out_ref
):
    mine = dot_nt(dv_ref[...], rotated_rows(w_ref, r2_ref))
    other = dot_nt(dv2_ref[...], rotated_rows(w2_ref, r22_ref))
    out_ref[0, 0:128, :] = (mine + other).astype(jnp.bfloat16)
    squares = sq_ref[...].astype(jnp.float32), sq2_ref[...].astype(jnp.float32)
    squares = [term[0:1] + term[1:2] + term[2:3] for term in squares]
    squares = jnp.concatenate([squares[0] + squares[1], jnp.zeros((1, 384), jnp.float32)], axis=1)
    scale = scale_ref[...]
    terms = three_terms(scale[:, :512]) + three_terms(scale[:, 512:]) + three_terms(squares)
    out_ref[0, 128:144, :] = in_rows(terms, 512)


def frame_pairs(core, weight, rotor, value_grad, scale, inputs, received):
    whole = pl.BlockSpec((128, 128), lambda i, core: (0, 0))
    sums = pl.BlockSpec((16, 128), lambda i, core: (144, 0))
    return pl.pallas_call(
        frame_kernel,
        grid_spec=pltpu.PrefetchScalarGridSpec(
            num_scalar_prefetch=1,
            grid=(4,),
            in_specs=[
                pl.BlockSpec((512, 128), lambda i, core: (i * 2 + core[0], 0)),
                whole,
                whole,
                pl.BlockSpec((512, 128), lambda i, core: (i, 0)),
                pl.BlockSpec((128, 128), lambda i, core: (16, 0)),
                pl.BlockSpec((128, 128), lambda i, core: (17, 0)),
                pl.BlockSpec((1, 1024), lambda i, core: (0, 0)),
                sums,
                sums,
            ],
            out_specs=pl.BlockSpec((1, 144, 512), lambda i, core: (i, 0, 0)),
        ),
        out_shape=jax.ShapeDtypeStruct((4, 144, 512), jnp.bfloat16),
        compiler_params=pltpu.CompilerParams(vmem_limit_bytes=BIG),
        cost_estimate=LONG,
        name="frame_pairs",
    )(core, weight, rotor, value_grad, received, received, received, scale, inputs, received)


def top_kernel(w_ref, r2_ref, top_ref):
    keep_top(top_ref, rotated_rows(w_ref, r2_ref))


def rotated_top(weight, rotor):
    return pl.pallas_call(
        top_kernel,
        grid=(4,),
        in_specs=[
            pl.BlockSpec((2048, 128), lambda i: (i, 0)),
            pl.BlockSpec((128, 128), lambda i: (0, 0)),
        ],
        out_specs=pl.BlockSpec((1, 128), lambda i: (0, 0)),
        out_shape=jax.ShapeDtypeStruct((1, 128), jnp.float32),
        compiler_params=pltpu.CompilerParams(vmem_limit_bytes=BIG),
        cost_estimate=CHEAP,
        name="rotated_top",
    )(weight, rotor)


def weight_grad_kernel(w_ref, r2_ref, top_ref, dv_ref, out_ref):
    step = top_ref[...] / 7.0 + SCALE_FLOOR
    rot = rotated_rows(w_ref, r2_ref).astype(jnp.float32)
    quant = soft_quant(rot, 1.0 / step, step * 7.0)
    out_ref[0] = dot_nt(dv_ref[...], quant.astype(jnp.bfloat16)).astype(jnp.bfloat16)


def weight_grad(weight, rotor, top, value_grad):
    small = pl.BlockSpec((128, 128), lambda i: (0, 0))
    row = pl.BlockSpec((1, 128), lambda i: (0, 0))
    return pl.pallas_call(
        weight_grad_kernel,
        grid=(8,),
        in_specs=[pl.BlockSpec((1024, 128), lambda i: (i, 0)), small, row, small],
        out_specs=pl.BlockSpec((1, 128, 1024), lambda i: (i, 0, 0)),
        out_shape=jax.ShapeDtypeStruct((8, 128, 1024), jnp.bfloat16),
        compiler_params=pltpu.CompilerParams(vmem_limit_bytes=BIG),
        cost_estimate=CHEAP,
        name="weight_grad",
    )(weight, rotor, top, value_grad)


def quant_kernel(core_ref, all_ref, term_ref, sum_ref, mask_ref, quant_ref, inv_ref):
    squares = jnp.sum(sum_ref[:, :, 0:128].astype(jnp.float32), axis=0)
    squares = squares[6:7] + squares[7:8] + squares[8:9]
    inverse = lax.rsqrt(squares / 8192.0 + NORM_EPS)
    inv_ref[...] = inverse
    inverse = jnp.transpose(jnp.broadcast_to(inverse, (128, 128)))
    mask = mask_ref[0]
    terms = term_ref[0].astype(jnp.float32)
    scale = jnp.concatenate(
        [terms[0:1] + terms[1:2] + terms[2:3], terms[3:4] + terms[4:5] + terms[5:6]], axis=1
    )
    recip = 1.0 / scale
    scale7 = scale * 7.0
    for lane in range(8):
        cols = slice(lane * 128, (lane + 1) * 128)
        normed = all_ref[0, 0:128, cols].astype(jnp.float32) * inverse
        soft = soft_quant(normed, recip[:, cols], scale7[:, cols])
        quant = jnp.where(mask[:, cols] > 0.0, normed, soft).astype(jnp.bfloat16)
        zh, zl, yh = lane // 4, (lane // 2) % 2, lane % 2
        place = zh * 2 + yh
        quant_ref[zl, :, place * 128 : (place + 1) * 128] = quant


def quantize(core, hidden_all, terms, mask):
    return pl.pallas_call(
        quant_kernel,
        grid_spec=pltpu.PrefetchScalarGridSpec(
            num_scalar_prefetch=1,
            grid=(4,),
            in_specs=[
                pl.BlockSpec((1, 128, 1024), lambda i, core: (i, 0, 0)),
                pl.BlockSpec((1, 16, 512), lambda i, core: (i, 8, 0)),
                pl.BlockSpec((4, 16, 512), lambda i, core: (0, 8, 0)),
                pl.BlockSpec((1, 1, 1024), lambda i, core: (i * 2 + core[0], 0, 0)),
            ],
            out_specs=[
                pl.BlockSpec((2, 128, 512), lambda i, core: (i, 0, 0)),
                pl.BlockSpec((1, 128), lambda i, core: (0, 0)),
            ],
        ),
        out_shape=[
            jax.ShapeDtypeStruct((8, 128, 512), jnp.bfloat16),
            jax.ShapeDtypeStruct((1, 128), jnp.float32),
        ],
        compiler_params=pltpu.CompilerParams(vmem_limit_bytes=BIG),
        cost_estimate=pl.CostEstimate(flops=17_250_000_000, bytes_accessed=1, transcendentals=0),
        name="quantize",
    )(core, hidden_all, terms, terms, mask)


def rotor_grad_kernel(core_ref, mine_ref, other_ref, wm_ref, wo_ref, dv_ref, r2_ref, total_ref):
    step = pl.program_id(0)
    total = jnp.zeros((128, 128), jnp.float32)
    for quant_ref, weight_ref in ((mine_ref, wm_ref), (other_ref, wo_ref)):
        for lane in range(8):
            zh, zl, yh = lane // 4, (lane // 2) % 2, lane % 2
            place = zh * 2 + yh
            total += jnp.dot(
                quant_ref[zl, :, place * 128 : (place + 1) * 128],
                weight_ref[0, lane * 128 : (lane + 1) * 128, :],
                preferred_element_type=jnp.float32,
            )

    @pl.when(step == 0)
    def _():
        total_ref[...] = total

    @pl.when(step > 0)
    def _():
        total_ref[...] += total

    @pl.when(step == 3)
    def _():
        r2_ref[...] = lax.dot_general(
            total_ref[...],
            dv_ref[...].astype(jnp.float32),
            (((0,), (0,)), ((), ())),
            precision=lax.Precision.HIGHEST,
            preferred_element_type=jnp.float32,
        )


def rotor_grad(core, mine, other, weight, value_grad):
    weight = weight.reshape(8, 1024, 128)
    quant_spec = pl.BlockSpec((2, 128, 512), lambda i, core: (i, 0, 0))
    return pl.pallas_call(
        rotor_grad_kernel,
        grid_spec=pltpu.PrefetchScalarGridSpec(
            num_scalar_prefetch=1,
            grid=(4,),
            in_specs=[
                quant_spec,
                quant_spec,
                pl.BlockSpec((1, 1024, 128), lambda i, core: (i * 2 + core[0], 0, 0)),
                pl.BlockSpec((1, 1024, 128), lambda i, core: (i * 2 + 1 - core[0], 0, 0)),
                pl.BlockSpec((128, 128), lambda i, core: (0, 0)),
            ],
            out_specs=pl.BlockSpec((128, 128), lambda i, core: (0, 0)),
            scratch_shapes=[pltpu.VMEM((128, 128), jnp.float32)],
        ),
        out_shape=jax.ShapeDtypeStruct((128, 128), jnp.float32),
        compiler_params=pltpu.CompilerParams(vmem_limit_bytes=BIG),
        cost_estimate=CHEAP,
        name="rotor_grad",
    )(core, mine, other, weight, weight, value_grad)


def outer_kernel(place_ref, frame_ref, quant_ref, *rest):
    out_ref, yh = rest[-1], place_ref[1]
    prod = lax.dot_general(
        frame_ref[...],
        quant_ref[...],
        (((0,), (0,)), ((), ())),
        preferred_element_type=jnp.float32,
    ).astype(jnp.bfloat16)
    for part in range(4):
        place = part // 2 * 2 + (part + yh) % 2
        out_ref[place] = prod[:, part * 128 : (part + 1) * 128]


def outer(place, frames, quants, into, name):
    more = [] if into is None else [into]
    return pl.pallas_call(
        outer_kernel,
        grid_spec=pltpu.PrefetchScalarGridSpec(
            num_scalar_prefetch=1,
            grid=(1,),
            in_specs=[
                pl.BlockSpec((1024, 512), lambda i, place: (0, 0)),
                pl.BlockSpec((1024, 512), lambda i, place: (0, 0)),
            ]
            + [pl.BlockSpec(memory_space=pl.ANY)] * len(more),
            out_specs=pl.BlockSpec((4, 512, 128), lambda i, place: (place[0], 0, 0)),
        ),
        out_shape=jax.ShapeDtypeStruct((8, 512, 128), jnp.bfloat16),
        input_output_aliases={3: 0} if more else {},
        compiler_params=pltpu.CompilerParams(vmem_limit_bytes=BIG),
        cost_estimate=CHEAP,
        name=name,
    )(place, frames, quants, *more)


def exchange(value, axes):
    return lax.all_to_all(value, axes, split_axis=0, concat_axis=0, tiled=True)


def shifted(value, axis, turn):
    count = lax.axis_size(axis)
    return lax.ppermute(value, axis, [(chip, (chip + turn) % count) for chip in range(count)])


def swap_core(value):
    return shifted(value, "c", 1)


def local(hidden_in, grad_sent, value_grad, value_weight, rotation, act_scale, outliers):
    sections = 64
    pairs = [(source, (source - 1) % sections) for source in range(sections)]
    core, yh = lax.axis_index("c"), lax.axis_index("yh")
    place = jnp.stack([core, yh]).astype(jnp.int32)
    other = jnp.stack([1 - core, yh]).astype(jnp.int32)
    wide = lambda value: value.astype(jnp.float32)
    tie = lax.optimization_barrier

    hidden_all = lax.all_gather(hidden_in, "yl", axis=0)

    inputs = core_inputs(place, hidden_in, value_weight, rotation, value_grad)
    received = swap_core(inputs)
    frame_pair = frame_pairs(
        place, value_weight, rotation, value_grad, act_scale, inputs, received
    )
    frame_pair, rotor = tie((frame_pair, rotation))
    frame_terms = exchange(frame_pair, "yl")
    top = rotated_top(value_weight, rotor)
    grad_parts = weight_grad(value_weight, rotor, top, value_grad)
    frame_terms, grad_parts = tie((frame_terms, grad_parts))
    frame = jnp.sum(wide(frame_terms[:, :128]), axis=0).astype(jnp.bfloat16)
    frames = exchange(jnp.broadcast_to(frame[None], (8, 128, 512)), NEAR).reshape(1024, 512)

    ids = outliers[0]
    blocks = (ids[None, :] // 128 == jnp.arange(64)[:, None]).astype(jnp.bfloat16)
    lanes = (ids[:, None] % 128 == jnp.arange(128)[None, :]).astype(jnp.bfloat16)
    mask = jnp.dot(blocks, lanes, preferred_element_type=jnp.float32).reshape(TP, 1, 1024)

    hidden_all, mask, grad_parts = tie((hidden_all, mask, grad_parts))
    grad_sum = lax.psum_scatter(grad_parts, TPA, scatter_dimension=0, tiled=False)
    quant, inverse = quantize(place, hidden_all, frame_terms, mask)
    frames, quant = tie((frames, quant))
    quants = exchange(quant, NEAR)
    quants, quant, grad_sent = tie((quants, quant, grad_sent))
    quants_other = swap_core(quants).reshape(1024, 512)
    incoming = lax.ppermute(grad_sent, SEC, pairs)
    parts = outer(place, frames, quants.reshape(1024, 512), None, "outer")
    parts = outer(other, frames, quants_other, parts, "outer_other")
    r2_grad = rotor_grad(place, quant, swap_core(quant), value_weight, value_grad)
    parts, r2_grad = tie((exchange(parts, "zh").reshape(4, 2, 512, 128), r2_grad))
    sums = jnp.sum(wide(parts), axis=0)
    r1_grad = sums[0] + wide(shifted(sums[1].astype(jnp.bfloat16), "yh", 1))

    mask_mine = lax.dynamic_index_in_dim(mask, lax.axis_index(TPA), 0, keepdims=False)
    inverse = inverse.reshape(128, 1)
    normed = wide(hidden_in) * inverse
    bounded = jnp.tanh(normed / (7.0 * act_scale))
    slope = jnp.where(mask_mine > 0.0, 1.0, 1.0 - bounded * bounded)
    emitted = (wide(incoming) + inverse * (wide(grad_sum) * slope)).astype(jnp.bfloat16)
    return (emitted, r1_grad, r2_grad)


def solution(mesh):
    fine = Mesh(mesh.devices.reshape(4, 4, 2, 2, 4, 2), SEC + TPA)
    both = P(SEC, TPA)
    in_specs = (both, both, both, both, both, both, P(SEC, None))
    out_specs = (both, P(TPA, SEC), both)
    return jax.shard_map(local, mesh=fine, in_specs=in_specs, out_specs=out_specs, check_vma=False)
```

```python
import math

import jax
import jax.numpy as jnp
from jax import lax
from jax.experimental import pallas as pl
from jax.experimental.pallas import tpu as pltpu
from jax.sharding import Mesh
from jax.sharding import PartitionSpec as P

ROWS_OUT = 4096
NORM_EPS = 1e-05
SCALE_FLOOR = 1e-06
TP = 8
BIG = 32 << 20
WHOLE = 60 << 20
CHEAP = pl.CostEstimate(flops=1, bytes_accessed=1, transcendentals=0)
LONG = pl.CostEstimate(flops=23_000_000_000, bytes_accessed=1, transcendentals=0)
SEC = ("x", "zh", "zl", "yh")
TPA = ("yl", "c")
NEAR = ("x", "zl")
FAR = ("zh", "yh")
SIN_POLY = (
    0.9999995827674866,
    -6.579691410064697,
    12.986435890197754,
    -12.188101768493652,
    6.558041572570801,
    -1.9530311822891235,
)


def soft_quant(values, inv_step, step7):
    scaled = values * inv_step
    turn = scaled - jnp.round(scaled)
    square = turn * turn
    poly = SIN_POLY[-1]
    for coef in SIN_POLY[-2::-1]:
        poly = poly * square + coef
    shifted = scaled - turn * poly
    return step7 * jnp.tanh(shifted * (1.0 / 7.0))


def dot_nt(left, right):
    return lax.dot_general(
        left, right, (((1,), (1,)), ((), ())), preferred_element_type=jnp.float32
    )


def prepare_kernel(x_ref, scale_ref, out_ref):
    scale = scale_ref[...]
    top = scale.astype(jnp.bfloat16).astype(jnp.float32)
    rest = scale - top
    mid = rest.astype(jnp.bfloat16).astype(jnp.float32)
    low = rest - mid
    row = lax.broadcasted_iota(jnp.int32, (16, scale.shape[1]), 0)
    extra = jnp.where(row == 0, top, jnp.where(row == 1, mid, jnp.where(row == 2, low, 0.0)))
    out_ref[0:128, :] = x_ref[...]
    out_ref[128:144, :] = extra.astype(jnp.bfloat16)


def prepare(hidden, scale):
    return pl.pallas_call(
        prepare_kernel,
        out_shape=jax.ShapeDtypeStruct((144, 1024), jnp.bfloat16),
        compiler_params=pltpu.CompilerParams(vmem_limit_bytes=BIG),
        cost_estimate=CHEAP,
        name="prepare",
    )(hidden, scale)


def rotated_rows(w_ref, r2_ref):
    rot = jnp.dot(w_ref[...], r2_ref[...], preferred_element_type=jnp.float32)
    return rot.astype(jnp.bfloat16)


def keep_top(top_ref, rot):
    step = pl.program_id(0)
    top = jnp.max(jnp.abs(rot.astype(jnp.float32)), axis=0, keepdims=True)

    @pl.when(step == 0)
    def _():
        top_ref[...] = top

    @pl.when(step > 0)
    def _():
        top_ref[...] = jnp.maximum(top_ref[...], top)


def frame_kernel(core_ref, w_ref, r2_ref, dv_ref, top_ref, keep_ref, send_ref):
    core = core_ref[0]
    rot = rotated_rows(w_ref, r2_ref)
    keep_top(top_ref, rot)
    for part in range(4):
        prod = dot_nt(dv_ref[...], rot[part * 512 : (part + 1) * 512]).astype(jnp.bfloat16)

        @pl.when(core == part % 2)
        def _():
            keep_ref[part // 2] = prod

        @pl.when(core != part % 2)
        def _():
            send_ref[part // 2] = prod


def frame_parts(core, weight, rotor, value_grad):
    whole = lambda i, core: (0, 0)
    half = jax.ShapeDtypeStruct((4, 128, 512), jnp.bfloat16)
    return pl.pallas_call(
        frame_kernel,
        grid_spec=pltpu.PrefetchScalarGridSpec(
            num_scalar_prefetch=1,
            grid=(2,),
            in_specs=[
                pl.BlockSpec((2048, 128), lambda i, core: (i, 0)),
                pl.BlockSpec((128, 128), whole),
                pl.BlockSpec((128, 128), whole),
            ],
            out_specs=[
                pl.BlockSpec((1, 128), whole),
                pl.BlockSpec((2, 128, 512), lambda i, core: (i, 0, 0)),
                pl.BlockSpec((2, 128, 512), lambda i, core: (i, 0, 0)),
            ],
        ),
        out_shape=[jax.ShapeDtypeStruct((1, 128), jnp.float32), half, half],
        compiler_params=pltpu.CompilerParams(vmem_limit_bytes=WHOLE),
        cost_estimate=LONG,
        name="frame_parts",
    )(core, weight, rotor, value_grad)


def top_kernel(w_ref, r2_ref, top_ref):
    keep_top(top_ref, rotated_rows(w_ref, r2_ref))


def rest_top(weight, rotor):
    return pl.pallas_call(
        top_kernel,
        grid=(2,),
        in_specs=[
            pl.BlockSpec((2048, 128), lambda i: (i + 2, 0)),
            pl.BlockSpec((128, 128), lambda i: (0, 0)),
        ],
        out_specs=pl.BlockSpec((1, 128), lambda i: (0, 0)),
        out_shape=jax.ShapeDtypeStruct((1, 128), jnp.float32),
        compiler_params=pltpu.CompilerParams(vmem_limit_bytes=BIG),
        cost_estimate=CHEAP,
        name="rest_top",
    )(weight, rotor)


def weight_grad_kernel(w_ref, r2_ref, one_ref, two_ref, dv_ref, out_ref):
    step = jnp.maximum(one_ref[...], two_ref[...]) / 7.0 + SCALE_FLOOR
    rot = rotated_rows(w_ref, r2_ref).astype(jnp.float32)
    quant = soft_quant(rot, 1.0 / step, step * 7.0)
    out_ref[0] = dot_nt(dv_ref[...], quant.astype(jnp.bfloat16)).astype(jnp.bfloat16)


def weight_grad(weight, rotor, top_one, top_two, value_grad):
    small = pl.BlockSpec((128, 128), lambda i: (0, 0))
    row = pl.BlockSpec((1, 128), lambda i: (0, 0))
    return pl.pallas_call(
        weight_grad_kernel,
        grid=(8,),
        in_specs=[pl.BlockSpec((1024, 128), lambda i: (i, 0)), small, row, row, small],
        out_specs=pl.BlockSpec((1, 128, 1024), lambda i: (i, 0, 0)),
        out_shape=jax.ShapeDtypeStruct((8, 128, 1024), jnp.bfloat16),
        compiler_params=pltpu.CompilerParams(vmem_limit_bytes=BIG),
        cost_estimate=CHEAP,
        name="weight_grad",
    )(weight, rotor, top_one, top_two, value_grad)


def quant_kernel(core_ref, all_ref, mask_ref, inv_ref, quant_ref):
    inverse = jnp.transpose(jnp.broadcast_to(inv_ref[...], (128, 128)))
    mask = mask_ref[0]
    scale = all_ref[0, 128:144, :].astype(jnp.float32)
    scale = scale[0:1] + scale[1:2] + scale[2:3]
    recip = 1.0 / scale
    scale7 = scale * 7.0
    for lane in range(8):
        cols = slice(lane * 128, (lane + 1) * 128)
        normed = all_ref[0, 0:128, cols].astype(jnp.float32) * inverse
        soft = soft_quant(normed, recip[:, cols], scale7[:, cols])
        quant = jnp.where(mask[:, cols] > 0.0, normed, soft).astype(jnp.bfloat16)
        zh, zl, yh = lane // 4, (lane // 2) % 2, lane % 2
        place = zh * 2 + yh
        quant_ref[zl, :, place * 128 : (place + 1) * 128] = quant


def quantize(core, hidden_all, mask, inverse):
    return pl.pallas_call(
        quant_kernel,
        grid_spec=pltpu.PrefetchScalarGridSpec(
            num_scalar_prefetch=1,
            grid=(4,),
            in_specs=[
                pl.BlockSpec((1, 144, 1024), lambda i, core: (i, 0, 0)),
                pl.BlockSpec((1, 1, 1024), lambda i, core: (i * 2 + core[0], 0, 0)),
                pl.BlockSpec((1, 128), lambda i, core: (0, 0)),
            ],
            out_specs=pl.BlockSpec((2, 128, 512), lambda i, core: (i, 0, 0)),
        ),
        out_shape=jax.ShapeDtypeStruct((8, 128, 512), jnp.bfloat16),
        compiler_params=pltpu.CompilerParams(vmem_limit_bytes=BIG),
        cost_estimate=pl.CostEstimate(flops=10_350_000_000, bytes_accessed=1, transcendentals=0),
        name="quantize",
    )(core, hidden_all, mask, inverse)


def rotor_grad_kernel(core_ref, mine_ref, other_ref, wm_ref, wo_ref, dv_ref, r2_ref, total_ref):
    step = pl.program_id(0)
    total = jnp.zeros((128, 128), jnp.float32)
    for quant_ref, weight_ref in ((mine_ref, wm_ref), (other_ref, wo_ref)):
        for lane in range(8):
            zh, zl, yh = lane // 4, (lane // 2) % 2, lane % 2
            place = zh * 2 + yh
            total += jnp.dot(
                quant_ref[zl, :, place * 128 : (place + 1) * 128],
                weight_ref[0, lane * 128 : (lane + 1) * 128, :],
                preferred_element_type=jnp.float32,
            )

    @pl.when(step == 0)
    def _():
        total_ref[...] = total

    @pl.when(step > 0)
    def _():
        total_ref[...] += total

    @pl.when(step == 3)
    def _():
        r2_ref[...] = lax.dot_general(
            total_ref[...],
            dv_ref[...].astype(jnp.float32),
            (((0,), (0,)), ((), ())),
            precision=lax.Precision.HIGHEST,
            preferred_element_type=jnp.float32,
        )


def rotor_grad(core, mine, other, weight, value_grad):
    weight = weight.reshape(8, 1024, 128)
    quant_spec = pl.BlockSpec((2, 128, 512), lambda i, core: (i, 0, 0))
    return pl.pallas_call(
        rotor_grad_kernel,
        grid_spec=pltpu.PrefetchScalarGridSpec(
            num_scalar_prefetch=1,
            grid=(4,),
            in_specs=[
                quant_spec,
                quant_spec,
                pl.BlockSpec((1, 1024, 128), lambda i, core: (i * 2 + core[0], 0, 0)),
                pl.BlockSpec((1, 1024, 128), lambda i, core: (i * 2 + 1 - core[0], 0, 0)),
                pl.BlockSpec((128, 128), lambda i, core: (0, 0)),
            ],
            out_specs=pl.BlockSpec((128, 128), lambda i, core: (0, 0)),
            scratch_shapes=[pltpu.VMEM((128, 128), jnp.float32)],
        ),
        out_shape=jax.ShapeDtypeStruct((128, 128), jnp.float32),
        compiler_params=pltpu.CompilerParams(vmem_limit_bytes=BIG),
        cost_estimate=CHEAP,
        name="rotor_grad",
    )(core, mine, other, weight, weight, value_grad)


def outer_kernel(place_ref, frame_ref, quant_ref, *rest):
    out_ref, yh = rest[-1], place_ref[1]
    prod = lax.dot_general(
        frame_ref[...],
        quant_ref[...],
        (((0,), (0,)), ((), ())),
        preferred_element_type=jnp.float32,
    ).astype(jnp.bfloat16)
    for part in range(2):
        out_ref[(part + yh) % 2] = prod[:, part * 128 : (part + 1) * 128]


def outer(place, frames, quants, into, name):
    more = [] if into is None else [into]
    return pl.pallas_call(
        outer_kernel,
        grid_spec=pltpu.PrefetchScalarGridSpec(
            num_scalar_prefetch=1,
            grid=(2,),
            in_specs=[
                pl.BlockSpec((1024, 512), lambda i, place: (0, 0)),
                pl.BlockSpec((1024, 256), lambda i, place: (0, i)),
            ]
            + [pl.BlockSpec(memory_space=pl.ANY)] * len(more),
            out_specs=pl.BlockSpec((2, 512, 128), lambda i, place: (place[0] * 2 + i, 0, 0)),
        ),
        out_shape=jax.ShapeDtypeStruct((8, 512, 128), jnp.bfloat16),
        input_output_aliases={3: 0} if more else {},
        compiler_params=pltpu.CompilerParams(vmem_limit_bytes=BIG),
        cost_estimate=CHEAP,
        name=name,
    )(place, frames, quants, *more)


def exchange(value, axes):
    return lax.all_to_all(value, axes, split_axis=0, concat_axis=0, tiled=True)


def shifted(value, axis, turn):
    count = lax.axis_size(axis)
    return lax.ppermute(value, axis, [(chip, (chip + turn) % count) for chip in range(count)])


def swap_core(value):
    return shifted(value, "c", 1)


def flipped(value, bit):
    return lax.ppermute(value, "yl", [(chip, chip ^ bit) for chip in range(4)])


def local(hidden_in, grad_sent, value_grad, value_weight, rotation, act_scale, outliers):
    sections = 64
    pairs = [(source, (source - 1) % sections) for source in range(sections)]
    core, yh = lax.axis_index("c"), lax.axis_index("yh")
    place = jnp.stack([core, yh]).astype(jnp.int32)
    other = jnp.stack([1 - core, yh]).astype(jnp.int32)
    wide = lambda value: value.astype(jnp.float32)
    tie = lax.optimization_barrier

    hidden_all = lax.all_gather(prepare(hidden_in, act_scale), "yl", axis=0)

    top_one, frame_keep, frame_send = frame_parts(place, value_weight, rotation, value_grad)
    frame_pair = (wide(frame_keep) + wide(swap_core(frame_send))).astype(jnp.bfloat16)
    frame_pair, hidden_two = tie((frame_pair, hidden_in))
    frame_terms = exchange(frame_pair, "yl")
    squares = jnp.sum(wide(hidden_two) * wide(hidden_two), axis=1).reshape(1, 128)
    squares = squares + swap_core(squares)
    squares = squares + flipped(squares, 1)
    squares = squares + flipped(squares, 2)
    inverse = lax.rsqrt(squares / 8192.0 + NORM_EPS)
    frame_terms, inverse, rotor = tie((frame_terms, inverse, rotation))
    frame = jnp.sum(wide(frame_terms), axis=0).astype(jnp.bfloat16)
    frames = exchange(jnp.broadcast_to(frame[None], (8, 128, 512)), NEAR).reshape(1024, 512)
    top_two = rest_top(value_weight, rotor)
    grad_parts = weight_grad(value_weight, rotor, top_one, top_two, value_grad)

    ids = outliers[0]
    blocks = (ids[None, :] // 128 == jnp.arange(64)[:, None]).astype(jnp.bfloat16)
    lanes = (ids[:, None] % 128 == jnp.arange(128)[None, :]).astype(jnp.bfloat16)
    mask = jnp.dot(blocks, lanes, preferred_element_type=jnp.float32).reshape(TP, 1, 1024)

    hidden_all, mask, grad_parts = tie((hidden_all, mask, grad_parts))
    grad_sum = lax.psum_scatter(grad_parts, TPA, scatter_dimension=0, tiled=False)
    quant = quantize(place, hidden_all, mask, inverse)
    frames, quant = tie((frames, quant))
    quants = exchange(quant, NEAR)
    r2_grad = rotor_grad(place, quant, swap_core(quant), value_weight, value_grad)
    quants, r2_grad, grad_sent = tie((quants, r2_grad, grad_sent))
    quants_other = swap_core(quants).reshape(1024, 512)
    incoming = lax.ppermute(grad_sent, SEC, pairs)
    parts = outer(place, frames, quants.reshape(1024, 512), None, "outer")
    parts = outer(other, frames, quants_other, parts, "outer_other")
    parts = exchange(parts, "zh").reshape(4, 2, 512, 128)
    sums = jnp.sum(wide(parts), axis=0)
    r1_grad = sums[0] + wide(shifted(sums[1].astype(jnp.bfloat16), "yh", 1))

    mask_mine = lax.dynamic_index_in_dim(mask, lax.axis_index(TPA), 0, keepdims=False)
    inverse = inverse.reshape(128, 1)
    normed = wide(hidden_in) * inverse
    bounded = jnp.tanh(normed / (7.0 * act_scale))
    slope = jnp.where(mask_mine > 0.0, 1.0, 1.0 - bounded * bounded)
    emitted = (wide(incoming) + inverse * (wide(grad_sum) * slope)).astype(jnp.bfloat16)
    return (emitted, r1_grad, r2_grad)


def solution(mesh):
    fine = Mesh(mesh.devices.reshape(4, 4, 2, 2, 4, 2), SEC + TPA)
    both = P(SEC, TPA)
    in_specs = (both, both, both, both, both, both, P(SEC, None))
    out_specs = (both, P(TPA, SEC), both)
    return jax.shard_map(local, mesh=fine, in_specs=in_specs, out_specs=out_specs, check_vma=False)
```
